256 devices in a mesh: replica: 32 (over z_hi, x, core), tensor: 8 (over z_lo, y).
Axes of the slice: x: 4, y: 4, z: 8 (z_hi: 4, z_lo: 2; z = z_hi * 2 + z_lo), core: 2. Of those that a mesh axis runs over, the one named last changes fastest.
Arguments:
- activations: bfloat16 [24576, 2048], P('replica'), may hold values from -6 to 6
- out_grads: bfloat16 [24576, 10240], P('replica', 'tensor'), may hold values from -0.21875 to 0.21875
- exponents: int32 [2048, 40], P(None, 'tensor'), may hold values from -6 to -3
- signs: int32 [10240], P('tensor'), may hold values from -1 to 1, as said below
- master: float32 [2048, 10240], P('replica', 'tensor'), may hold values from -0.006 to 0.006
- moment: float32 [2048, 10240], P('replica', 'tensor'), may hold values from -0.06 to 0.06
- second: float32 [2048, 10240], P('replica', 'tensor'), may hold values from 0.01 to 0.03
Outputs:
- grad_mean: float32 [2048, 10240], P('replica', 'tensor')
- moment_new: float32 [2048, 10240], P('replica', 'tensor')
- second_new: float32 [2048, 10240], P('replica', 'tensor')
- master_new: float32 [2048, 10240], P('replica', 'tensor')
- weights: bfloat16 [2048, 10240], P(None, 'tensor')
The draws below stay inside these ranges and needn't reach their ends.
Inputs may be any that keep to these rules, and one draw needn't show every extreme that they name: `signs`: every entry is -1 or +1.
All inputs are finite; a program needn't handle non-finite values.
Results may differ from the reference program's by a relative error of at most 0.018.
Values may be sent and summed in bfloat16 or wider, within the bound.
No kernel may reach another device: no remote copies, remote signals or barrier semaphores. Data moves between devices by JAX's collectives and lax.ppermute only.
A program may use at most 64 MiB of HBM per device.

```python
import math
import jax
import jax.numpy as jnp
import numpy as np
from jax import lax

TILE = 256
TOK_DEV = 768
QKV_COLS = 10240
ROWS = 2048
TOKENS = 24576
N_REPLICA = 32


def draw_signs(key, part):
    key = jax.random.fold_in(key, 7)
    coins = jax.random.randint(key, (QKV_COLS,), 0, 2)
    return (2 * coins - 1).astype(jnp.int32)


def place_ends(values, rng, low, largest):
    shape = values.shape
    place = [jax.random.randint(jax.random.fold_in(rng, axis), (), 0, shape[axis]) for axis in range(len(shape))]
    values = values.at[tuple(place)].set(low)
    longest = shape.index(max(shape))
    place[longest] = (place[longest] + 1) % shape[longest]
    return values.at[tuple(place)].set(largest)


def spiked(drawn, own_key, source, target, blocks, factor):
    owner, partner = [(jnp.arange(drawn.shape[position]) // (drawn.shape[position] // blocks)).reshape([-1 if axis == position else 1 for axis in range(drawn.ndim)]) for position in (source, target)]
    chosen = jax.random.permutation(own_key, blocks)[partner]
    strong = (owner == chosen) | (owner == (partner + blocks // 2) % blocks)
    return jnp.where(strong, factor * drawn, drawn)


def level_of(stream_key, shape, cuts, least, high):
    factor_of = 1.0
    for dim, parts in cuts:
        draws = jax.random.uniform(jax.random.fold_in(jax.random.fold_in(stream_key, 6), dim), (parts,), jnp.float32, least / len(cuts), high / len(cuts))
        factor_of = factor_of * jnp.repeat(jnp.exp(draws), shape[dim] // parts).reshape((-1,) + (1,) * (len(shape) - 1 - dim))
    return factor_of


def gaussian(stream_key, shape, width, reach, cuts=(), held_as=jnp.bfloat16):
    entries = jax.random.normal(stream_key, shape, jnp.float32) * width
    if len(cuts) > 0:
        entries = level_of(stream_key, shape, cuts, -0.22, 0.18) * entries
    return jnp.clip(entries, min=-reach, max=reach).astype(held_as)


def gaussian_with(own_key, shape, spread, reach, split, heavy, held_as=jnp.bfloat16):
    array = spread * jax.random.normal(own_key, shape, jnp.float32)
    if split:
        array = array * level_of(own_key, shape, split, -0.22, 0.18)
    return jnp.clip(spiked(array, jax.random.fold_in(own_key, 3), *heavy), -reach, reach).astype(held_as)


def setup_inputs(seed: int = 0) -> dict:
    key_list = jax.random.split(jax.random.key(seed), 8)
    return {
        "activations": gaussian_with(key_list[0], (TOKENS, ROWS), 1.0, 6.0, ((0, 32),), (0, 1, 32, 2.75)),
        "out_grads": gaussian(key_list[1], (TOKENS, QKV_COLS), TOK_DEV ** -0.5, 0.21875, ((0, 32), (1, 8))),
        "exponents": place_ends(jax.random.randint(key_list[2], (ROWS, QKV_COLS // TILE), -6, -2), jax.random.fold_in(key_list[2], 1), -6, (-2) - 1).astype(jnp.int32),
        "signs": draw_signs(jax.random.fold_in(key_list[7], 71), 0),
        "master": gaussian(key_list[4], (ROWS, QKV_COLS), 0.001, 0.006, ((0, 32), (1, 8)), jnp.float32),
        "moment": gaussian(key_list[5], (ROWS, QKV_COLS), 0.01, 0.06, ((0, 32), (1, 8)), jnp.float32),
        "second": jnp.clip(jnp.exp(math.log(0.03) - 1.0986123 * jax.random.uniform(key_list[6], (ROWS, QKV_COLS), jnp.float32) ** level_of(key_list[6], (ROWS, QKV_COLS), ((0, 32), (1, 8)), -0.2, 0.2)), 0.01, 0.03),
    }


beta_one = 0.9
beta_two = 0.95
epsilon = 1e-08
decay_rate = 0.1
learn_rate = 0.001
step_number = 100.0

def hadamard_table(order):
    positions = np.arange(order)
    intersection = positions[:, None] & positions[None, :]
    parity = np.zeros((order, order))
    for level in range(order.bit_length()):
        parity = parity + intersection // 2 ** level % 2
    return np.where(parity % 2 == 0, 1.0, -1.0) / math.sqrt(order)

def reference(activations, out_grads, exponents, signs, master, moment, second):
    tile_count = QKV_COLS // TILE
    table = jnp.asarray(hadamard_table(TILE), jnp.float32)
    sign_float = signs.astype(jnp.float32)
    expanded = jnp.repeat(exponents.astype(jnp.float32), TILE, axis=1)
    shrink = jnp.exp2(-expanded)
    growth = jnp.exp2(expanded)

    def per_replica(running, index):
        window = lax.dynamic_slice_in_dim(activations, (index * TOK_DEV).astype(jnp.int32), TOK_DEV, 0)
        grads = lax.dynamic_slice_in_dim(out_grads, (index * TOK_DEV).astype(jnp.int32), TOK_DEV, 0)
        partial_value = jnp.dot(window.T, grads, preferred_element_type=jnp.float32).astype(jnp.bfloat16)
        flipped = (partial_value.astype(jnp.float32) * sign_float).astype(jnp.bfloat16).astype(jnp.float32)
        rotated = jnp.einsum('rtk,kj->rtj', flipped.reshape(ROWS, tile_count, TILE), table).reshape(ROWS, QKV_COLS)
        quant = jnp.clip(rotated * shrink, -127.0, 127.0).astype(jnp.bfloat16)
        return (running + quant.astype(jnp.float32), None)
    summed, _ = lax.scan(per_replica, jnp.zeros((ROWS, QKV_COLS), jnp.float32), jnp.arange(N_REPLICA, dtype=jnp.int32))
    decoded = summed * growth
    restored = jnp.einsum('rtk,kj->rtj', decoded.reshape(ROWS, tile_count, TILE), table, precision=lax.Precision.HIGHEST).reshape(ROWS, QKV_COLS)
    grad_mean = restored * sign_float / N_REPLICA
    moment_new = beta_one * moment + (1.0 - beta_one) * grad_mean
    second_new = beta_two * second + (1.0 - beta_two) * grad_mean * grad_mean
    first_fix = 1.0 - beta_one ** step_number
    second_fix = 1.0 - beta_two ** step_number
    update = moment_new / first_fix / (jnp.sqrt(second_new / second_fix) + epsilon) + decay_rate * master
    master_new = master - learn_rate * update
    weights = master_new.astype(jnp.bfloat16)
    return (grad_mean, moment_new, second_new, master_new, weights)
```

```python
import functools
import math

import jax
import jax.numpy as jnp
import numpy as np
from jax import lax
from jax.experimental import pallas as pl
from jax.experimental.pallas import tpu as pltpu
from jax.sharding import PartitionSpec as P

TILE = 256
NZ, NX, NC = 4, 4, 2
ROW = 64
COLS = 1280
COLS_A = 896
COLS_B = COLS - COLS_A
TOK = 768

beta_one = 0.9
beta_two = 0.95
epsilon = 1e-08
decay_rate = 0.1
learn_rate = 0.001
step_number = 100.0

F32 = jnp.float32
BF = jnp.bfloat16


def hadamard_table(order):
    positions = np.arange(order)
    intersection = positions[:, None] & positions[None, :]
    parity = np.zeros((order, order))
    for level in range(order.bit_length()):
        parity = parity + intersection // 2**level % 2
    return np.where(parity % 2 == 0, 1.0, -1.0) / math.sqrt(order)


def replica_perm(dz=0, dx=0, dc=0):
    pairs = []
    for z in range(NZ):
        for x in range(NX):
            for c in range(NC):
                to = (((z + dz) % NZ) * NX + (x + dx) % NX) * NC + (c + dc) % NC
                pairs.append(((z * NX + x) * NC + c, to))
    return pairs


def send(value, **shift):
    return lax.ppermute(value, "replica", replica_perm(**shift))


def quant_kernel(first, width, meta, act, grads, exps, signs, table, mine, theirs, rotated):
    @pl.when(pl.program_id(0) == 0)
    def _():
        lo = first // TILE
        for tile in range(lo, -(-(first + width) // TILE)):
            flipped = grads[:, tile * TILE : (tile + 1) * TILE] * signs[
                :, tile * TILE : (tile + 1) * TILE
            ].astype(BF)
            turned = jnp.dot(flipped, table[...], preferred_element_type=F32).astype(BF)
            a = max(first, tile * TILE)
            b = min(first + width, (tile + 1) * TILE)
            rotated[:, a - first : b - first] = turned[:, a - tile * TILE : b - tile * TILE]

    total = lax.dot_general(
        act[...], rotated[...], (((0,), (0,)), ((), ())), preferred_element_type=F32
    )
    shrink = jnp.exp2(-exps[...].astype(F32))
    core = meta[2]
    for tile in range(first // TILE, -(-(first + width) // TILE)):
        a = max(first, tile * TILE) - first
        b = min(first + width, (tile + 1) * TILE) - first
        part = jnp.clip(total[:, a:b] * shrink[:, tile : tile + 1], -127.0, 127.0).astype(BF)
        top, bottom = part[:ROW], part[ROW:]
        mine[0, 0, :, a:b] = jnp.where(core == 0, top, bottom)
        theirs[0, 0, :, a:b] = jnp.where(core == 0, bottom, top)


def quantized(first, width, x_outer, meta, act, grads, exps, signs, table):
    def group(i, meta):
        if x_outer:
            dx, dz = i // NZ, lax.rem(i, NZ)
        else:
            dz, dx = i // NX, lax.rem(i, NX)
        return lax.rem(meta[0] + dz, NZ) * NX + lax.rem(meta[1] + dx, NX)

    out = jax.ShapeDtypeStruct((4, 4, ROW, width), BF)
    out_spec = pl.BlockSpec((1, 1, ROW, width), lambda i, meta: (i // 4, lax.rem(i, 4), 0, 0))
    return pl.pallas_call(
        functools.partial(quant_kernel, first, width),
        grid_spec=pltpu.PrefetchScalarGridSpec(
            num_scalar_prefetch=1,
            grid=(NZ * NX,),
            in_specs=[
                pl.BlockSpec((TOK, 2 * ROW), lambda i, meta: (0, group(i, meta))),
                pl.BlockSpec((TOK, COLS), lambda i, meta: (0, 0)),
                pl.BlockSpec((2 * ROW, COLS // TILE), lambda i, meta: (group(i, meta), 0)),
                pl.BlockSpec((1, COLS), lambda i, meta: (0, 0)),
                pl.BlockSpec((TILE, TILE), lambda i, meta: (0, 0)),
            ],
            out_specs=[out_spec, out_spec],
            scratch_shapes=[pltpu.VMEM((TOK, width), BF)],
        ),
        out_shape=[out, out],
        compiler_params=pltpu.CompilerParams(vmem_limit_bytes=32 * 1024 * 1024),
        name="quantize",
    )(meta, act, grads, exps, signs, table)


def pair_kernel(mine, other, *outs):
    for k, out in enumerate(outs):
        out[...] = (mine[k].astype(F32) + other[k].astype(F32)).astype(BF)


def pair_sum(mine, other):
    width = mine.shape[-1]
    spec = pl.BlockSpec((4, 1, ROW, width), lambda i: (0, i, 0, 0))
    return pl.pallas_call(
        pair_kernel,
        grid=(4,),
        in_specs=[spec, spec],
        out_specs=[pl.BlockSpec((1, ROW, width), lambda i: (i, 0, 0))] * 4,
        out_shape=[jax.ShapeDtypeStruct((4, ROW, width), BF)] * 4,
        name="pair_sum",
    )(mine, other)


def quad_kernel(a, b, c, d, *outs):
    for k, out in enumerate(outs):
        out[...] = (
            (a[k].astype(F32) + b[k].astype(F32)) + (c[k].astype(F32) + d[k].astype(F32))
        ).astype(BF)


def quad_sum(parts):
    width = parts[0].shape[-1]
    return pl.pallas_call(
        quad_kernel,
        out_shape=[jax.ShapeDtypeStruct((ROW, width), BF)] * 4,
        name="quad_sum",
    )(*parts)


def update_kernel(*refs):
    a = refs[0:4]
    b = refs[4:8]
    exps, signs, table, master, moment, second = refs[8:14]
    grad_out, moment_out, second_out, master_out, weights_a, weights_b = refs[14:20]
    total_a = (a[0][...].astype(F32) + a[1][...].astype(F32)) + (
        a[2][...].astype(F32) + a[3][...].astype(F32)
    )
    total_b = (b[0][...].astype(F32) + b[1][...].astype(F32)) + (
        b[2][...].astype(F32) + b[3][...].astype(F32)
    )
    total = jnp.concatenate([total_a, total_b], axis=1)
    growth = jnp.exp2(exps[...].astype(F32))
    first_fix = 1.0 - beta_one**step_number
    second_fix = 1.0 - beta_two**step_number
    for tile in range(COLS // TILE):
        cut = slice(tile * TILE, (tile + 1) * TILE)
        decoded = total[:, cut] * growth[:, tile : tile + 1]
        high = decoded.astype(BF)
        rest = decoded - high.astype(F32)
        middle = rest.astype(BF)
        low = (rest - middle.astype(F32)).astype(BF)
        restored = jnp.dot(high, table[...], preferred_element_type=F32) + (
            jnp.dot(middle, table[...], preferred_element_type=F32)
            + jnp.dot(low, table[...], preferred_element_type=F32)
        )
        grad = restored * (signs[:, cut].astype(F32) * (1.0 / (NZ * NX * NC)))
        moment_new = beta_one * moment[:, cut] + (1.0 - beta_one) * grad
        second_new = beta_two * second[:, cut] + (1.0 - beta_two) * grad * grad
        update = (
            moment_new / first_fix / (jnp.sqrt(second_new / second_fix) + epsilon)
            + decay_rate * master[:, cut]
        )
        master_new = master[:, cut] - learn_rate * update
        grad_out[:, cut] = grad
        moment_out[:, cut] = moment_new
        second_out[:, cut] = second_new
        master_out[:, cut] = master_new
        weights = master_new.astype(BF)
        if (tile + 1) * TILE <= COLS_A:
            weights_a[:, cut] = weights
        elif tile * TILE >= COLS_A:
            weights_b[:, tile * TILE - COLS_A : (tile + 1) * TILE - COLS_A] = weights
        else:
            weights_a[:, tile * TILE : COLS_A] = weights[:, : COLS_A - tile * TILE]
            weights_b[:, : (tile + 1) * TILE - COLS_A] = weights[:, COLS_A - tile * TILE :]


def updated(parts_a, parts_b, exps, signs, table, master, moment, second):
    full = jax.ShapeDtypeStruct((ROW, COLS), F32)
    return pl.pallas_call(
        update_kernel,
        out_shape=[
            full,
            full,
            full,
            full,
            jax.ShapeDtypeStruct((ROW, COLS_A), BF),
            jax.ShapeDtypeStruct((ROW, COLS_B), BF),
        ],
        compiler_params=pltpu.CompilerParams(vmem_limit_bytes=32 * 1024 * 1024),
        name="update",
    )(*parts_a, *parts_b, exps, signs, table, master, moment, second)


def place_kernel(meta, *refs):
    pieces, out, sems = refs[:-2], refs[-2], refs[-1]
    zh, x, core = meta[0], meta[1], meta[2]
    copies = []
    for k, piece in enumerate(pieces):
        other, rest = k // 8, k % 8
        is_b, outer = rest // 4, rest % 4
        row_core = jnp.where(other == 1, 1 - core, core)
        for inner in range(4):
            dx, dz = (inner, outer) if is_b else (outer, inner)
            z_from = lax.rem(zh + NZ - dz, NZ)
            x_from = lax.rem(x + NX - dx, NX)
            row = pl.multiple_of(((z_from * NX + x_from) * NC + row_core) * ROW, ROW)
            cut = pl.ds(COLS_A, COLS_B) if is_b else pl.ds(0, COLS_A)
            copies.append(
                pltpu.make_async_copy(
                    piece.at[inner], out.at[pl.ds(row, ROW), cut], sems.at[len(copies)]
                )
            )
    for copy in copies:
        copy.start()
    for copy in copies:
        copy.wait()


def placed(meta, pieces):
    return pl.pallas_call(
        place_kernel,
        in_specs=[pl.BlockSpec(memory_space=pltpu.SMEM)]
        + [pl.BlockSpec(memory_space=pl.ANY)] * len(pieces),
        out_specs=pl.BlockSpec(memory_space=pl.ANY),
        out_shape=jax.ShapeDtypeStruct((NZ * NX * NC * ROW, COLS), BF),
        scratch_shapes=[pltpu.SemaphoreType.DMA((4 * len(pieces),))],
        name="place",
    )(meta, *pieces)


def on_device(activations, out_grads, exponents, signs, master, moment, second):
    table = jnp.asarray(hadamard_table(TILE), BF)
    replica = lax.axis_index("replica")
    zh, x, core = replica // (NX * NC), lax.rem(replica // NC, NX), lax.rem(replica, NC)
    meta = jnp.stack([zh, x, core]).astype(jnp.int32)
    sign_row = signs.reshape(1, COLS)
    own_exps = lax.dynamic_slice_in_dim(exponents, replica * ROW, ROW, 0)

    args = (meta, activations, out_grads, exponents, sign_row, table)
    mine_a, theirs_a = quantized(0, COLS_A, True, *args)
    other_a = send(theirs_a, dc=1)
    mine_b, theirs_b = quantized(COLS_A, COLS_B, False, *args)
    other_b = send(theirs_b, dc=1)
    a = pair_sum(mine_a, other_a)
    a = quad_sum([a[0], send(a[1], dx=1), send(a[3], dx=3), send(a[2], dx=2)])
    b = pair_sum(mine_b, other_b)
    b = quad_sum([b[0], send(b[1], dz=1), send(b[3], dz=3), send(b[2], dz=2)])
    a = [a[0], send(a[1], dz=1), send(a[3], dz=3), send(a[2], dz=2)]
    b = [b[0], send(b[1], dx=1), send(b[3], dx=3), send(b[2], dx=2)]
    grad_mean, moment_new, second_new, master_new, wa, wb = updated(
        a, b, own_exps, sign_row, table, master, moment, second
    )
    wa = jnp.stack([wa] + [send(wa, dz=k) for k in (1, 2, 3)])
    wb = jnp.stack([wb] + [send(wb, dx=k) for k in (1, 2, 3)])
    ga = [wa] + [send(wa, dx=k) for k in (1, 2, 3)]
    gb = [wb] + [send(wb, dz=k) for k in (1, 2, 3)]
    own = ga + gb
    other = [send(piece, dc=1) for piece in own]
    weights = placed(meta, own + other)
    return (grad_mean, moment_new, second_new, master_new, weights)


def solution(mesh):
    in_specs = (
        P("replica", None),
        P("replica", "tensor"),
        P(None, "tensor"),
        P("tensor"),
        P("replica", "tensor"),
        P("replica", "tensor"),
        P("replica", "tensor"),
    )
    out_specs = (
        P("replica", "tensor"),
        P("replica", "tensor"),
        P("replica", "tensor"),
        P("replica", "tensor"),
        P(None, "tensor"),
    )
    return jax.shard_map(
        on_device, mesh=mesh, in_specs=in_specs, out_specs=out_specs, check_vma=False
    )
```

```python
import functools
import math

import jax
import jax.numpy as jnp
import numpy as np
from jax import lax
from jax.experimental import pallas as pl
from jax.experimental.pallas import tpu as pltpu
from jax.sharding import PartitionSpec as P

TILE = 256
NZ, NX, NC = 4, 4, 2
REPLICAS = NZ * NX * NC
ROW = 64
GROUP = NC * ROW
ROWS = NZ * NX * GROUP
COLS = 1280
TILES = COLS // TILE
TOK = 768

beta_one = 0.9
beta_two = 0.95
epsilon = 1e-08
decay_rate = 0.1
learn_rate = 0.001
step_number = 100.0

F32 = jnp.float32
BF = jnp.bfloat16
MIB = 1024 * 1024
HBM = pl.BlockSpec(memory_space=pltpu.HBM)
FULL = pl.BlockSpec(memory_space=pltpu.VMEM)

SIDES = ((1, 1), (3, 1), (1, 2), (3, 2), (1, 3), (3, 3))
CORNERS = ((2, 1), (2, 3), (2, 2))
REST = ((0, 1), (0, 2), (0, 3), (1, 0), (2, 0), (3, 0), (0, 0))


def hadamard_table(order):
    positions = np.arange(order)
    intersection = positions[:, None] & positions[None, :]
    parity = np.zeros((order, order))
    for level in range(order.bit_length()):
        parity = parity + intersection // 2**level % 2
    return np.where(parity % 2 == 0, 1.0, -1.0) / math.sqrt(order)


def replica_perm(dx, dz, dc):
    pairs = []
    for z in range(NZ):
        for x in range(NX):
            for c in range(NC):
                to = (((z + dz) % NZ) * NX + (x + dx) % NX) * NC + (c + dc) % NC
                pairs.append(((z * NX + x) * NC + c, to))
    return pairs


def send(value, dx=0, dz=0, dc=0):
    return lax.ppermute(value, "replica", replica_perm(dx, dz, dc))


def place_of():
    replica = lax.axis_index("replica")
    return replica // (NX * NC), lax.rem(replica // NC, NX), lax.rem(replica, NC)


def vmem(*shape, dtype=BF):
    return pltpu.VMEM(shape, dtype)


def held(*arrays):
    return [pltpu.with_memory_space_constraint(a, pltpu.VMEM) for a in arrays]


def far(*arrays):
    return [pltpu.with_memory_space_constraint(a, pltpu.HBM) for a in arrays]


TINY = pl.CostEstimate(flops=1, bytes_accessed=1, transcendentals=0)


def params(mib):
    return pltpu.CompilerParams(vmem_limit_bytes=mib * MIB)


def quant_group(dx, dz, act, rotated, exps, mine, theirs, k):
    zh, x, core = place_of()
    group = lax.rem(zh + dz, NZ) * NX + lax.rem(x + dx, NX)
    lanes = pl.ds(pl.multiple_of(group * GROUP, GROUP), GROUP)
    total = lax.dot_general(
        act[:, lanes], rotated[...], (((0,), (0,)), ((), ())), preferred_element_type=F32
    )
    shrink = jnp.exp2(-exps[:, lanes].astype(F32)).T
    for tile in range(TILES):
        cut = slice(tile * TILE, (tile + 1) * TILE)
        part = jnp.clip(total[:, cut] * shrink[:, tile : tile + 1], -127.0, 127.0).astype(BF)
        top, bottom = part[:ROW], part[ROW:]
        mine[k, :, cut] = jnp.where(core == 0, top, bottom)
        theirs[k, :, cut] = jnp.where(core == 0, bottom, top)


def first_kernel(
    act_far, grads_far, exps_far, signs_far, table_far,
    mine, theirs, act, rotated, exps, signs, table,
    grads, line, sems,
):
    zh, _, _ = place_of()
    small = [
        pltpu.make_async_copy(signs_far, line, sems.at[0]),
        pltpu.make_async_copy(table_far, table, sems.at[1]),
        pltpu.make_async_copy(exps_far, exps, sems.at[2]),
    ]
    tiles = []
    for tile in range(TILES):
        cut = pl.ds(tile * TILE, TILE)
        tiles.append(
            pltpu.make_async_copy(grads_far.at[:, cut], grads.at[:, cut], sems.at[3 + tile])
        )
    quarters = []
    for dz in (1, 2, 3, 0):
        lanes = pl.ds(pl.multiple_of(lax.rem(zh + dz, NZ) * (ROWS // NZ), ROWS // NZ), ROWS // NZ)
        quarters.append(
            pltpu.make_async_copy(
                act_far.at[:, lanes], act.at[:, lanes], sems.at[3 + TILES + len(quarters)]
            )
        )
    for copy in small + tiles:
        copy.start()
    for copy in small:
        copy.wait()
    signs[...] = line[...].reshape(1, COLS)
    for tile in range(TILES):
        cut = slice(tile * TILE, (tile + 1) * TILE)
        tiles[tile].wait()
        if tile < len(quarters):
            quarters[tile].start()
        flipped = grads[:, cut] * signs[:, cut].astype(BF)
        rotated[:, cut] = jnp.dot(flipped, table[...], preferred_element_type=F32).astype(BF)
    for k, (dx, dz) in enumerate(SIDES):
        if k % 2 == 0:
            quarters[k // 2].wait()
        quant_group(dx, dz, act, rotated, exps, mine, theirs, k)
    quarters[3].wait()


def quantized_first(act, grads, exps, signs, table):
    n = len(SIDES)
    return pl.pallas_call(
        first_kernel,
        in_specs=[HBM] * 5,
        out_specs=[FULL] * 7,
        out_shape=[
            vmem(n, ROW, COLS),
            vmem(n, ROW, COLS),
            vmem(TOK, ROWS),
            vmem(TOK, COLS),
            vmem(TILES, ROWS, dtype=jnp.int32),
            vmem(1, COLS, dtype=jnp.int32),
            vmem(TILE, TILE),
        ],
        scratch_shapes=[
            pltpu.VMEM((TOK, COLS), BF),
            pltpu.VMEM((COLS,), jnp.int32),
            pltpu.SemaphoreType.DMA((7 + TILES,)),
        ],
        compiler_params=params(12),
        cost_estimate=TINY,
        name="quantize_sides",
    )(*far(act, grads, exps, signs, table))


def next_kernel(blocks, act, rotated, exps, _, mine, theirs):
    for k, (dx, dz) in enumerate(blocks):
        quant_group(dx, dz, act, rotated, exps, mine, theirs, k)


def quantized_next(blocks, act, rotated, exps, after):
    n = len(blocks)
    return pl.pallas_call(
        functools.partial(next_kernel, blocks),
        in_specs=[FULL] * 4,
        out_specs=[FULL] * 2,
        out_shape=[vmem(n, ROW, COLS)] * 2,
        compiler_params=params(8),
        cost_estimate=TINY,
        name="quantize_more",
    )(*held(act, rotated, exps, after))


def add(*parts):
    total = parts[0].astype(F32)
    for part in parts[1:]:
        total = total + part.astype(F32)
    return total.astype(BF)


def sides_kernel(mine, other, _b, _c, right, left):
    for k, (dx, dz) in enumerate(SIDES):
        out = right if dx == 1 else left
        out[dz - 1] = add(mine[k], other[k])


def sides_sum(mine, other, *after):
    return pl.pallas_call(
        sides_kernel,
        in_specs=[FULL] * 4,
        out_specs=[FULL] * 2,
        out_shape=[vmem(NZ - 1, ROW, COLS)] * 2,
        compiler_params=params(4),
        cost_estimate=TINY,
        name="sides_sum",
    )(*held(mine, other, *after))


def corners_kernel(mine, other, mine_rest, other_rest, *outs):
    for k, out in enumerate(outs[:3]):
        out[...] = add(mine[k], other[k])
    for k in range(len(REST)):
        outs[3][k] = add(mine_rest[k], other_rest[k])


def corners_sum(*parts):
    return pl.pallas_call(
        corners_kernel,
        in_specs=[FULL] * 4,
        out_specs=[FULL] * 4,
        out_shape=[vmem(ROW, COLS)] * 3 + [vmem(len(REST), ROW, COLS)],
        compiler_params=params(4),
        cost_estimate=TINY,
        name="corners_sum",
    )(*held(*parts))


def middle_kernel(pairs, left, right, below, above, across, *outs):
    z1, z2, z3, x1, x2, x3, own = outs
    for k, out in enumerate((z1, z2, z3)):
        more = (across[...],) if k == 1 else ()
        out[...] = add(pairs[k], left[k], right[k], *more)
    x1[...] = pairs[3]
    x2[...] = add(pairs[4], below[...], above[...])
    x3[...] = pairs[5]
    own[...] = pairs[6]


def middle_sum(*parts):
    return pl.pallas_call(
        middle_kernel,
        in_specs=[FULL] * 6,
        out_specs=[FULL] * 7,
        out_shape=[vmem(ROW, COLS)] * 7,
        compiler_params=params(4),
        cost_estimate=TINY,
        name="middle_sum",
    )(*held(*parts))


def update_kernel(*refs):
    parts = refs[0:7]
    exps, signs, table, master, moment, second = refs[7:13]
    grad_out, moment_out, second_out, master_out, weights_out = refs[13:18]
    zh, x, core = place_of()
    lanes = pl.ds(pl.multiple_of((zh * NX + x) * GROUP, GROUP), GROUP)
    growth = jnp.exp2(exps[:, lanes].astype(F32)).T
    growth = jnp.where(core == 0, growth[:ROW], growth[ROW:])
    first_fix = 1.0 - beta_one**step_number
    second_fix = 1.0 - beta_two**step_number
    for tile in range(TILES):
        cut = slice(tile * TILE, (tile + 1) * TILE)
        total = parts[0][:, cut].astype(F32)
        for part in parts[1:]:
            total = total + part[:, cut].astype(F32)
        decoded = total * growth[:, tile : tile + 1]
        high = decoded.astype(BF)
        rest = decoded - high.astype(F32)
        middle = rest.astype(BF)
        low = (rest - middle.astype(F32)).astype(BF)
        restored = jnp.dot(high, table[...], preferred_element_type=F32) + (
            jnp.dot(middle, table[...], preferred_element_type=F32)
            + jnp.dot(low, table[...], preferred_element_type=F32)
        )
        grad = restored * (signs[:, cut].astype(F32) * (1.0 / REPLICAS))
        moment_new = beta_one * moment[:, cut] + (1.0 - beta_one) * grad
        second_new = beta_two * second[:, cut] + (1.0 - beta_two) * grad * grad
        update = (
            moment_new / first_fix / (jnp.sqrt(second_new / second_fix) + epsilon)
            + decay_rate * master[:, cut]
        )
        master_new = master[:, cut] - learn_rate * update
        weights_out[:, cut] = master_new.astype(BF)
        grad_out[:, cut] = grad
        moment_out[:, cut] = moment_new
        second_out[:, cut] = second_new
        master_out[:, cut] = master_new


def updated(parts, exps, signs, table, state):
    return pl.pallas_call(
        update_kernel,
        in_specs=[FULL] * 13,
        out_specs=[FULL] * 5,
        out_shape=[vmem(ROW, COLS, dtype=F32)] * 4 + [vmem(ROW, COLS)],
        compiler_params=params(4),
        cost_estimate=TINY,
        name="update",
    )(*held(*parts, exps, signs, table, *state))


def join_kernel(count, *refs):
    out = refs[-1]
    row = 0
    for part in refs[:count]:
        if len(part.shape) == 3:
            out[row : row + part.shape[0]] = part[...]
            row += part.shape[0]
        else:
            out[row] = part[...]
            row += 1


def joined(*parts, after=()):
    blocks = sum(part.shape[0] if part.ndim == 3 else 1 for part in parts)
    return pl.pallas_call(
        functools.partial(join_kernel, len(parts)),
        in_specs=[FULL] * (len(parts) + len(after)),
        out_specs=FULL,
        out_shape=vmem(blocks, ROW, COLS),
        compiler_params=params(2),
        cost_estimate=TINY,
        name="join",
    )(*held(*parts, *after))


def fan_kernel(w, x3, x1, x2, z2, z3, z1, column, row, corner, first):
    for k, part in enumerate((z1, z3, z2)):
        column[k] = part[...]
    row[...] = x2[...]
    corner[...] = z2[...]
    for k, part in enumerate((w, z1, z3, z2, x2, x1, x3)):
        first[k] = part[...]


def fanned(*parts):
    return pl.pallas_call(
        fan_kernel,
        in_specs=[FULL] * 7,
        out_specs=[FULL] * 4,
        out_shape=[vmem(3, ROW, COLS), vmem(ROW, COLS), vmem(ROW, COLS), vmem(7, ROW, COLS)],
        compiler_params=params(2),
        cost_estimate=TINY,
        name="fan",
    )(*held(*parts))


def place_kernel(names, count, chained, *refs):
    pieces = refs[:2]
    state = refs[2 : 2 + count]
    out = refs[2 + count + chained]
    state_out = refs[3 + count + chained : 3 + 2 * count + chained]
    token, sems = refs[-2:]
    token[...] = jnp.zeros_like(token)
    zh, x, core = place_of()
    copies = []
    for flip, piece in enumerate(pieces):
        row_core = 1 - core if flip else core
        for k, (dx, dz) in enumerate(names):
            z_from = lax.rem(zh + NZ - dz, NZ)
            x_from = lax.rem(x + NX - dx, NX)
            row = pl.multiple_of(((z_from * NX + x_from) * NC + row_core) * ROW, ROW)
            copies.append(
                pltpu.make_async_copy(
                    piece.at[k], out.at[pl.ds(row, ROW), :], sems.at[len(copies)]
                )
            )
    for near, away in zip(state, state_out):
        copies.append(pltpu.make_async_copy(near, away, sems.at[len(copies)]))
    for copy in copies:
        copy.start()
    for copy in copies:
        copy.wait()


def placed(names, mine, other, state, previous):
    count = len(state)
    chained = previous is not None
    full = jax.ShapeDtypeStruct((ROW, COLS), F32)
    return pl.pallas_call(
        functools.partial(place_kernel, names, count, chained),
        in_specs=[FULL] * (2 + count) + [HBM] * chained,
        out_specs=[HBM] * (1 + count) + [FULL],
        out_shape=[jax.ShapeDtypeStruct((ROWS, COLS), BF)] + [full] * count + [vmem(16, 128)],
        input_output_aliases={2 + count: 0} if chained else {},
        scratch_shapes=[pltpu.SemaphoreType.DMA((2 * len(names) + count,))],
        compiler_params=params(2),
        cost_estimate=TINY,
        name="place",
    )(*held(mine, other, *state), *((previous,) if chained else ()))


def on_device(activations, out_grads, exponents, signs, master, moment, second):
    table = jnp.asarray(hadamard_table(TILE), BF)
    mine_a, theirs_a, act, rotated, exps, sign_row, table = quantized_first(
        activations, out_grads, exponents.T, signs, table
    )
    other_a = send(theirs_a, dc=1)
    mine_b, theirs_b = quantized_next(CORNERS, act, rotated, exps, theirs_a)
    other_b = send(theirs_b, dc=1)
    mine_c, theirs_c = quantized_next(REST, act, rotated, exps, theirs_b)
    other_c = send(theirs_c, dc=1)
    right, left = sides_sum(mine_a, other_a, mine_b, mine_c)
    from_left, from_right = send(right, dx=1), send(left, dx=3)
    up, down, across, pairs = corners_sum(mine_b, other_b, mine_c, other_c)
    from_below, from_above = send(up, dz=1), send(down, dz=3)
    from_across = send(across, dx=2)
    z1, z2, z3, x1, x2, x3, own = middle_sum(
        pairs, from_left, from_right, from_below, from_above, from_across
    )
    parts = [
        own,
        send(z1, dz=1),
        send(z3, dz=3),
        send(z2, dz=2),
        send(x2, dx=2),
        send(x1, dx=1),
        send(x3, dx=3),
    ]
    *state_new, w = updated(parts, exps, sign_row, table, (master, moment, second))

    x3, x1, x2 = send(w, dx=3), send(w, dx=1), send(w, dx=2)
    z2, z3, z1 = send(w, dz=2), send(w, dz=3), send(w, dz=1)
    column, row, corner, first = fanned(w, x3, x1, x2, z2, z3, z1)
    other_first = send(first, dc=1)
    x2f = send(corner, dx=2)
    z3f, z1f = send(row, dz=3), send(row, dz=1)
    x3c, x1c = send(column, dx=3), send(column, dx=1)
    names = ((0, 0), (0, 1), (0, 3), (0, 2), (2, 0), (1, 0), (3, 0))
    weights, *state_new, token = placed(names, first, other_first, state_new, None)
    last = joined(x2f, z3f, z1f, x3c, x1c, after=(token,))
    names = ((2, 2), (2, 3), (2, 1), (3, 1), (3, 3), (3, 2), (1, 1), (1, 3), (1, 2))
    weights, _ = placed(names, last, send(last, dc=1), (), weights)
    return (*state_new, weights)


def solution(mesh):
    in_specs = (
        P("replica", None),
        P("replica", "tensor"),
        P(None, "tensor"),
        P("tensor"),
        P("replica", "tensor"),
        P("replica", "tensor"),
        P("replica", "tensor"),
    )
    out_specs = (
        P("replica", "tensor"),
        P("replica", "tensor"),
        P("replica", "tensor"),
        P("replica", "tensor"),
        P(None, "tensor"),
    )
    return jax.shard_map(
        on_device, mesh=mesh, in_specs=in_specs, out_specs=out_specs, check_vma=False
    )
```

```python
import functools
import math

import jax
import jax.numpy as jnp
import numpy as np
from jax import lax
from jax.experimental import pallas as pl
from jax.experimental.pallas import tpu as pltpu
from jax.sharding import PartitionSpec as P

TILE = 256
NZ, NX, NC = 4, 4, 2
REPLICAS = NZ * NX * NC
ROW = 64
GROUP = NC * ROW
ROWS = NZ * NX * GROUP
COLS = 1280
TILES = COLS // TILE
TOK = 768

beta_one = 0.9
beta_two = 0.95
epsilon = 1e-08
decay_rate = 0.1
learn_rate = 0.001
step_number = 100.0

F32 = jnp.float32
BF = jnp.bfloat16
MIB = 1024 * 1024
HBM = pl.BlockSpec(memory_space=pltpu.HBM)
FULL = pl.BlockSpec(memory_space=pltpu.VMEM)

SIDES = ((1, 1), (3, 1), (1, 2), (3, 2), (1, 3), (3, 3))
CORNERS = ((2, 1), (2, 3), (2, 2))
REST = ((0, 1), (0, 2), (0, 3), (1, 0), (2, 0), (3, 0), (0, 0))


def hadamard_table(order):
    positions = np.arange(order)
    intersection = positions[:, None] & positions[None, :]
    parity = np.zeros((order, order))
    for level in range(order.bit_length()):
        parity = parity + intersection // 2**level % 2
    return np.where(parity % 2 == 0, 1.0, -1.0) / math.sqrt(order)


def replica_perm(dx, dz, dc):
    pairs = []
    for z in range(NZ):
        for x in range(NX):
            for c in range(NC):
                to = (((z + dz) % NZ) * NX + (x + dx) % NX) * NC + (c + dc) % NC
                pairs.append(((z * NX + x) * NC + c, to))
    return pairs


def send(value, dx=0, dz=0, dc=0):
    return lax.ppermute(value, "replica", replica_perm(dx, dz, dc))


def place_of():
    replica = lax.axis_index("replica")
    return replica // (NX * NC), lax.rem(replica // NC, NX), lax.rem(replica, NC)


def vmem(*shape, dtype=BF):
    return pltpu.VMEM(shape, dtype)


def held(*arrays):
    return [pltpu.with_memory_space_constraint(a, pltpu.VMEM) for a in arrays]


def far(*arrays):
    return [pltpu.with_memory_space_constraint(a, pltpu.HBM) for a in arrays]


TINY = pl.CostEstimate(flops=1, bytes_accessed=1, transcendentals=0)


def params(mib):
    return pltpu.CompilerParams(vmem_limit_bytes=mib * MIB)


def quant_group(dx, dz, act, rotated, exps, mine, theirs, k):
    zh, x, core = place_of()
    group = lax.rem(zh + dz, NZ) * NX + lax.rem(x + dx, NX)
    lanes = pl.ds(pl.multiple_of(group * GROUP, GROUP), GROUP)
    total = lax.dot_general(
        act[:, lanes], rotated[...], (((0,), (0,)), ((), ())), preferred_element_type=F32
    )
    shrink = jnp.exp2(-exps[:, lanes].astype(F32)).T
    for tile in range(TILES):
        cut = slice(tile * TILE, (tile + 1) * TILE)
        part = jnp.clip(total[:, cut] * shrink[:, tile : tile + 1], -127.0, 127.0).astype(BF)
        top, bottom = part[:ROW], part[ROW:]
        mine[k, :, cut] = jnp.where(core == 0, top, bottom)
        theirs[k, :, cut] = jnp.where(core == 0, bottom, top)


def first_kernel(
    act_far, grads_far, exps_far, signs_far, table_far,
    mine, theirs, act, rotated, exps, signs, table,
    grads, line, sems,
):
    small = [
        pltpu.make_async_copy(signs_far, line, sems.at[0]),
        pltpu.make_async_copy(table_far, table, sems.at[1]),
        pltpu.make_async_copy(exps_far, exps, sems.at[2]),
    ]
    strips = []
    for far_ref, near, count in ((grads_far, grads, 3), (act_far, act, 4)):
        for k in range(count):
            rows = pl.ds(k * TOK // count, TOK // count)
            strips.append(
                pltpu.make_async_copy(far_ref.at[rows], near.at[rows], sems.at[3 + len(strips)])
            )
    for copy in small + strips:
        copy.start()
    for copy in small:
        copy.wait()
    signs[...] = line[...].reshape(1, COLS)
    for k in range(3):
        rows = slice(k * TOK // 3, (k + 1) * TOK // 3)
        strips[k].wait()
        for tile in range(TILES):
            cut = slice(tile * TILE, (tile + 1) * TILE)
            flipped = grads[rows, cut] * signs[:, cut].astype(BF)
            turned = jnp.dot(flipped, table[...], preferred_element_type=F32)
            rotated[rows, cut] = turned.astype(BF)
    for copy in strips[3:]:
        copy.wait()
    for k, (dx, dz) in enumerate(SIDES):
        quant_group(dx, dz, act, rotated, exps, mine, theirs, k)


def quantized_first(act, grads, exps, signs, table):
    n = len(SIDES)
    return pl.pallas_call(
        first_kernel,
        in_specs=[HBM] * 5,
        out_specs=[FULL] * 7,
        out_shape=[
            vmem(n, ROW, COLS),
            vmem(n, ROW, COLS),
            vmem(TOK, ROWS),
            vmem(TOK, COLS),
            vmem(TILES, ROWS, dtype=jnp.int32),
            vmem(1, COLS, dtype=jnp.int32),
            vmem(TILE, TILE),
        ],
        scratch_shapes=[
            pltpu.VMEM((TOK, COLS), BF),
            pltpu.VMEM((COLS,), jnp.int32),
            pltpu.SemaphoreType.DMA((10,)),
        ],
        compiler_params=params(12),
        cost_estimate=TINY,
        name="quantize_sides",
    )(*far(act, grads, exps, signs, table))


def next_kernel(blocks, act, rotated, exps, _, mine, theirs):
    for k, (dx, dz) in enumerate(blocks):
        quant_group(dx, dz, act, rotated, exps, mine, theirs, k)


def quantized_next(blocks, act, rotated, exps, after):
    n = len(blocks)
    return pl.pallas_call(
        functools.partial(next_kernel, blocks),
        in_specs=[FULL] * 4,
        out_specs=[FULL] * 2,
        out_shape=[vmem(n, ROW, COLS)] * 2,
        compiler_params=params(8),
        cost_estimate=TINY,
        name="quantize_more",
    )(*held(act, rotated, exps, after))


def add(*parts):
    total = parts[0].astype(F32)
    for part in parts[1:]:
        total = total + part.astype(F32)
    return total.astype(BF)


def sides_kernel(mine, other, _b, _c, right, left):
    for k, (dx, dz) in enumerate(SIDES):
        out = right if dx == 1 else left
        out[dz - 1] = add(mine[k], other[k])


def sides_sum(mine, other, *after):
    return pl.pallas_call(
        sides_kernel,
        in_specs=[FULL] * 4,
        out_specs=[FULL] * 2,
        out_shape=[vmem(NZ - 1, ROW, COLS)] * 2,
        compiler_params=params(4),
        cost_estimate=TINY,
        name="sides_sum",
    )(*held(mine, other, *after))


def corners_kernel(mine, other, mine_rest, other_rest, *outs):
    for k, out in enumerate(outs[:3]):
        out[...] = add(mine[k], other[k])
    for k in range(len(REST)):
        outs[3][k] = add(mine_rest[k], other_rest[k])


def corners_sum(*parts):
    return pl.pallas_call(
        corners_kernel,
        in_specs=[FULL] * 4,
        out_specs=[FULL] * 4,
        out_shape=[vmem(ROW, COLS)] * 3 + [vmem(len(REST), ROW, COLS)],
        compiler_params=params(4),
        cost_estimate=TINY,
        name="corners_sum",
    )(*held(*parts))


def middle_kernel(pairs, left, right, below, above, across, *outs):
    z1, z2, z3, x1, x2, x3, own = outs
    for k, out in enumerate((z1, z2, z3)):
        more = (across[...],) if k == 1 else ()
        out[...] = add(pairs[k], left[k], right[k], *more)
    x1[...] = pairs[3]
    x2[...] = add(pairs[4], below[...], above[...])
    x3[...] = pairs[5]
    own[...] = pairs[6]


def middle_sum(*parts):
    return pl.pallas_call(
        middle_kernel,
        in_specs=[FULL] * 6,
        out_specs=[FULL] * 7,
        out_shape=[vmem(ROW, COLS)] * 7,
        compiler_params=params(4),
        cost_estimate=TINY,
        name="middle_sum",
    )(*held(*parts))


def seen_kernel(*refs):
    refs[-1][...] = jnp.zeros_like(refs[-1])


def seen(*parts):
    return pl.pallas_call(
        seen_kernel,
        in_specs=[FULL] * len(parts),
        out_specs=FULL,
        out_shape=vmem(16, 128),
        compiler_params=params(1),
        cost_estimate=TINY,
        name="seen",
    )(*held(*parts))


def update_kernel(*refs):
    parts = refs[0:7]
    exps, signs, table, master, moment, second = refs[7:13]
    grad_out, moment_out, second_out, master_out, weights_out = refs[14:19]
    zh, x, core = place_of()
    lanes = pl.ds(pl.multiple_of((zh * NX + x) * GROUP, GROUP), GROUP)
    growth = jnp.exp2(exps[:, lanes].astype(F32)).T
    growth = jnp.where(core == 0, growth[:ROW], growth[ROW:])
    first_fix = 1.0 - beta_one**step_number
    second_fix = 1.0 - beta_two**step_number
    for tile in range(TILES):
        cut = slice(tile * TILE, (tile + 1) * TILE)
        total = parts[0][:, cut].astype(F32)
        for part in parts[1:]:
            total = total + part[:, cut].astype(F32)
        decoded = total * growth[:, tile : tile + 1]
        high = decoded.astype(BF)
        rest = decoded - high.astype(F32)
        middle = rest.astype(BF)
        low = (rest - middle.astype(F32)).astype(BF)
        restored = jnp.dot(high, table[...], preferred_element_type=F32) + (
            jnp.dot(middle, table[...], preferred_element_type=F32)
            + jnp.dot(low, table[...], preferred_element_type=F32)
        )
        grad = restored * (signs[:, cut].astype(F32) * (1.0 / REPLICAS))
        moment_new = beta_one * moment[:, cut] + (1.0 - beta_one) * grad
        second_new = beta_two * second[:, cut] + (1.0 - beta_two) * grad * grad
        update = (
            moment_new / first_fix / (jnp.sqrt(second_new / second_fix) + epsilon)
            + decay_rate * master[:, cut]
        )
        master_new = master[:, cut] - learn_rate * update
        weights_out[:, cut] = master_new.astype(BF)
        grad_out[:, cut] = grad
        moment_out[:, cut] = moment_new
        second_out[:, cut] = second_new
        master_out[:, cut] = master_new


def updated(parts, exps, signs, table, state, after):
    return pl.pallas_call(
        update_kernel,
        in_specs=[FULL] * 14,
        out_specs=[FULL] * 5,
        out_shape=[vmem(ROW, COLS, dtype=F32)] * 4 + [vmem(ROW, COLS)],
        compiler_params=params(4),
        cost_estimate=TINY,
        name="update",
    )(*held(*parts, exps, signs, table, *state, after))


def join_kernel(count, *refs):
    out = refs[-1]
    row = 0
    for part in refs[:count]:
        if len(part.shape) == 3:
            out[row : row + part.shape[0]] = part[...]
            row += part.shape[0]
        else:
            out[row] = part[...]
            row += 1


def joined(*parts, after=()):
    blocks = sum(part.shape[0] if part.ndim == 3 else 1 for part in parts)
    return pl.pallas_call(
        functools.partial(join_kernel, len(parts)),
        in_specs=[FULL] * (len(parts) + len(after)),
        out_specs=FULL,
        out_shape=vmem(blocks, ROW, COLS),
        compiler_params=params(2),
        cost_estimate=TINY,
        name="join",
    )(*held(*parts, *after))


def fan_kernel(w, x3, x1, x2, z2, z3, z1, _, column, row, corner, first):
    for k, part in enumerate((z1, z3, z2)):
        column[k] = part[...]
    row[...] = x2[...]
    corner[...] = z2[...]
    for k, part in enumerate((w, z1, z3, z2, x2, x1, x3)):
        first[k] = part[...]


def fanned(*parts):
    return pl.pallas_call(
        fan_kernel,
        in_specs=[FULL] * 8,
        out_specs=[FULL] * 4,
        out_shape=[vmem(3, ROW, COLS), vmem(ROW, COLS), vmem(ROW, COLS), vmem(7, ROW, COLS)],
        compiler_params=params(2),
        cost_estimate=TINY,
        name="fan",
    )(*held(*parts))


def place_kernel(names, flips, count, chained, *refs):
    pieces = refs[: len(flips)]
    refs = refs[len(flips) :]
    state = refs[:count]
    out = refs[count + chained]
    state_out = refs[1 + count + chained : 1 + 2 * count + chained]
    token, sems = refs[-2:]
    token[...] = jnp.zeros_like(token)
    zh, x, core = place_of()
    copies = []
    for flip, piece in zip(flips, pieces):
        row_core = 1 - core if flip else core
        for k, (dx, dz) in enumerate(names):
            z_from = lax.rem(zh + NZ - dz, NZ)
            x_from = lax.rem(x + NX - dx, NX)
            row = pl.multiple_of(((z_from * NX + x_from) * NC + row_core) * ROW, ROW)
            copies.append(
                pltpu.make_async_copy(
                    piece.at[k], out.at[pl.ds(row, ROW), :], sems.at[len(copies)]
                )
            )
    for near, away in zip(state, state_out):
        copies.append(pltpu.make_async_copy(near, away, sems.at[len(copies)]))
    for copy in copies:
        copy.start()
    for copy in copies:
        copy.wait()


def placed(names, flips, pieces, state, previous):
    count = len(state)
    chained = previous is not None
    full = jax.ShapeDtypeStruct((ROW, COLS), F32)
    return pl.pallas_call(
        functools.partial(place_kernel, names, flips, count, chained),
        in_specs=[FULL] * (len(flips) + count) + [HBM] * chained,
        out_specs=[HBM] * (1 + count) + [FULL],
        out_shape=[jax.ShapeDtypeStruct((ROWS, COLS), BF)] + [full] * count + [vmem(16, 128)],
        input_output_aliases={len(flips) + count: 0} if chained else {},
        scratch_shapes=[pltpu.SemaphoreType.DMA((len(flips) * len(names) + count,))],
        compiler_params=params(2),
        cost_estimate=TINY,
        name="place",
    )(*held(*pieces, *state), *((previous,) if chained else ()))


def on_device(activations, out_grads, exponents, signs, master, moment, second):
    table = jnp.asarray(hadamard_table(TILE), BF)
    mine_a, theirs_a, act, rotated, exps, sign_row, table = quantized_first(
        activations, out_grads, exponents.T, signs, table
    )
    other_a = send(theirs_a, dc=1)
    mine_b, theirs_b = quantized_next(CORNERS, act, rotated, exps, theirs_a)
    other_b = send(theirs_b, dc=1)
    mine_c, theirs_c = quantized_next(REST, act, rotated, exps, theirs_b)
    other_c = send(theirs_c, dc=1)
    right, left = sides_sum(mine_a, other_a, mine_b, mine_c)
    from_left, from_right = send(right, dx=1), send(left, dx=3)
    up, down, across, pairs = corners_sum(mine_b, other_b, mine_c, other_c)
    from_below, from_above = send(up, dz=1), send(down, dz=3)
    from_across = send(across, dx=2)
    z1, z2, z3, x1, x2, x3, own = middle_sum(
        pairs, from_left, from_right, from_below, from_above, from_across
    )
    parts = [
        own,
        send(z1, dz=1),
        send(z3, dz=3),
        send(z2, dz=2),
        send(x2, dx=2),
        send(x1, dx=1),
        send(x3, dx=3),
    ]
    token = seen(parts[3], parts[4], seen(parts[1], parts[2]))
    state = (master, moment, second)
    *state_new, w = updated(parts, exps, sign_row, table, state, token)

    x3, x1, x2 = send(w, dx=3), send(w, dx=1), send(w, dx=2)
    z2, z3, z1 = send(w, dz=2), send(w, dz=3), send(w, dz=1)
    token = seen(z2, x2, seen(z1, z3))
    column, row, corner, first = fanned(w, x3, x1, x2, z2, z3, z1, token)
    other_first = send(first, dc=1)
    x2f = send(corner, dx=2)
    z3f, z1f = send(row, dz=3), send(row, dz=1)
    x3c, x1c = send(column, dx=3), send(column, dx=1)
    names = ((0, 0), (0, 1), (0, 3), (0, 2), (2, 0), (1, 0), (3, 0))
    weights, *state_new, token = placed(
        names, (False, True), (first, other_first), state_new, None
    )
    last = joined(x2f, z3f, z1f, x3c, x1c, after=(token,))
    names = ((2, 2), (2, 3), (2, 1), (3, 1), (3, 3), (3, 2), (1, 1), (1, 3), (1, 2))
    other_last = send(last, dc=1)
    weights, _ = placed(names, (False,), (last,), (), weights)
    weights, _ = placed(names, (True,), (other_last,), (), weights)
    return (*state_new, weights)


def solution(mesh):
    in_specs = (
        P("replica", None),
        P("replica", "tensor"),
        P(None, "tensor"),
        P("tensor"),
        P("replica", "tensor"),
        P("replica", "tensor"),
        P("replica", "tensor"),
    )
    out_specs = (
        P("replica", "tensor"),
        P("replica", "tensor"),
        P("replica", "tensor"),
        P("replica", "tensor"),
        P(None, "tensor"),
    )
    return jax.shard_map(
        on_device, mesh=mesh, in_specs=in_specs, out_specs=out_specs, check_vma=False
    )
```

```python
import functools
import math

import jax
import jax.numpy as jnp
import numpy as np
from jax import lax
from jax.experimental import pallas as pl
from jax.experimental.pallas import tpu as pltpu
from jax.sharding import PartitionSpec as P

TILE = 256
NZ, NX, NC = 4, 4, 2
REPLICAS = NZ * NX * NC
ROW = 64
GROUP = NC * ROW
ROWS = NZ * NX * GROUP
COLS = 1280
TILES = COLS // TILE
TOK = 768

beta_one = 0.9
beta_two = 0.95
epsilon = 1e-08
decay_rate = 0.1
learn_rate = 0.001
step_number = 100.0

F32 = jnp.float32
BF = jnp.bfloat16
MIB = 1024 * 1024
HBM = pl.BlockSpec(memory_space=pltpu.HBM)
FULL = pl.BlockSpec(memory_space=pltpu.VMEM)

FIRST_NAMES = ((0, 0), (0, "a"), (0, 2), (2, 0), ("a", 0), ("b", 0))
LAST_NAMES = ((0, "b"), ("a", "b"), ("b", "b"), (2, "b"))
LAST_NAMES += ((2, "a"), (2, 2), ("b", "a"), ("b", 2), ("a", "a"), ("a", 2))


def hadamard_table(order):
    positions = np.arange(order)
    intersection = positions[:, None] & positions[None, :]
    parity = np.zeros((order, order))
    for level in range(order.bit_length()):
        parity = parity + intersection // 2**level % 2
    return np.where(parity % 2 == 0, 1.0, -1.0) / math.sqrt(order)


def step(way, core):
    if way == "a":
        return 1 + 2 * core
    if way == "b":
        return 3 - 2 * core
    return way


def replica_perm(dx, dz, dc):
    pairs = []
    for z in range(NZ):
        for x in range(NX):
            for c in range(NC):
                z_to, x_to = (z + step(dz, c)) % NZ, (x + step(dx, c)) % NX
                pairs.append(((z * NX + x) * NC + c, (z_to * NX + x_to) * NC + (c + dc) % NC))
    return pairs


def send(value, dx=0, dz=0, dc=0):
    return lax.ppermute(value, "replica", replica_perm(dx, dz, dc))


def place_of():
    replica = lax.axis_index("replica")
    return replica // (NX * NC), lax.rem(replica // NC, NX), lax.rem(replica, NC)


def vmem(*shape, dtype=BF):
    return pltpu.VMEM(shape, dtype)


def held(*arrays):
    return [pltpu.with_memory_space_constraint(a, pltpu.VMEM) for a in arrays]


def far(*arrays):
    return [pltpu.with_memory_space_constraint(a, pltpu.HBM) for a in arrays]


TINY = pl.CostEstimate(flops=1, bytes_accessed=1, transcendentals=0)


def params(mib):
    return pltpu.CompilerParams(vmem_limit_bytes=mib * MIB)


def quant_group(dx, dz, act, rotated, exps, mine, theirs):
    zh, x, core = place_of()
    group = lax.rem(zh + dz, NZ) * NX + lax.rem(x + dx, NX)
    lanes = pl.ds(pl.multiple_of(group * GROUP, GROUP), GROUP)
    total = lax.dot_general(
        act[:, lanes], rotated[...], (((0,), (0,)), ((), ())), preferred_element_type=F32
    )
    shrink = jnp.exp2(-exps[:, lanes].astype(F32)).T
    for tile in range(TILES):
        cut = slice(tile * TILE, (tile + 1) * TILE)
        part = jnp.clip(total[:, cut] * shrink[:, tile : tile + 1], -127.0, 127.0).astype(BF)
        top, bottom = part[:ROW], part[ROW:]
        mine[:, cut] = jnp.where(core == 0, top, bottom)
        theirs[:, cut] = jnp.where(core == 0, bottom, top)


def first_kernel(
    act_far, grads_far, exps_far, signs_far, table_far,
    mine, theirs, act, rotated, exps, signs, table,
    grads, line, sems,
):
    small = [
        pltpu.make_async_copy(signs_far, line, sems.at[0]),
        pltpu.make_async_copy(table_far, table, sems.at[1]),
        pltpu.make_async_copy(exps_far, exps, sems.at[2]),
    ]
    strips = []
    for far_ref, near, count in ((grads_far, grads, 3), (act_far, act, 4)):
        for k in range(count):
            rows = pl.ds(k * TOK // count, TOK // count)
            strips.append(
                pltpu.make_async_copy(far_ref.at[rows], near.at[rows], sems.at[3 + len(strips)])
            )
    for copy in small + strips:
        copy.start()
    for copy in small:
        copy.wait()
    signs[...] = line[...].reshape(1, COLS)
    for k in range(3):
        rows = slice(k * TOK // 3, (k + 1) * TOK // 3)
        strips[k].wait()
        for tile in range(TILES):
            cut = slice(tile * TILE, (tile + 1) * TILE)
            flipped = grads[rows, cut] * signs[:, cut].astype(BF)
            turned = jnp.dot(flipped, table[...], preferred_element_type=F32)
            rotated[rows, cut] = turned.astype(BF)
    for copy in strips[3:]:
        copy.wait()
    _, _, core = place_of()
    for dx in range(NX):
        here, there = mine.at[dx], theirs.at[NX + dx]
        quant_group(dx, step("a", core), act, rotated, exps, here, there)
        here, there = mine.at[NX + dx], theirs.at[dx]
        quant_group(dx, step("b", core), act, rotated, exps, here, there)


def quantized_first(act, grads, exps, signs, table):
    return pl.pallas_call(
        first_kernel,
        in_specs=[HBM] * 5,
        out_specs=[FULL] * 7,
        out_shape=[vmem(2 * NX, ROW, COLS)] * 2
        + [
            vmem(TOK, ROWS),
            vmem(TOK, COLS),
            vmem(TILES, ROWS, dtype=jnp.int32),
            vmem(1, COLS, dtype=jnp.int32),
            vmem(TILE, TILE),
        ],
        scratch_shapes=[
            pltpu.VMEM((TOK, COLS), BF),
            pltpu.VMEM((COLS,), jnp.int32),
            pltpu.SemaphoreType.DMA((10,)),
        ],
        compiler_params=params(12),
        cost_estimate=TINY,
        name="quantize_first",
    )(*far(act, grads, exps, signs, table))


def next_kernel(dz, act, rotated, exps, _, mine, theirs):
    for dx in range(NX):
        quant_group(dx, dz, act, rotated, exps, mine.at[dx], theirs.at[dx])


def quantized_next(dz, act, rotated, exps, after):
    return pl.pallas_call(
        functools.partial(next_kernel, dz),
        in_specs=[FULL] * 4,
        out_specs=[FULL] * 2,
        out_shape=[vmem(NX, ROW, COLS)] * 2,
        compiler_params=params(8),
        cost_estimate=TINY,
        name="quantize_next",
    )(*held(act, rotated, exps, after))


def add(*parts):
    total = parts[0].astype(F32)
    for part in parts[1:]:
        total = total + part.astype(F32)
    return total.astype(BF)


def row_kernel(mine, other, _, out):
    for k in range(NX):
        out[k] = add(mine[k], other[k])


def row_sum(mine, other, after):
    return pl.pallas_call(
        row_kernel,
        in_specs=[FULL] * 3,
        out_specs=FULL,
        out_shape=vmem(NX, ROW, COLS),
        compiler_params=params(2),
        cost_estimate=TINY,
        name="row_sum",
    )(*held(mine, other, after))


def sides_kernel(mine, other, mine_2, other_2, mine_0, other_0, xa, xb, x2, pairs):
    _, _, core = place_of()
    a, b = step("a", core), step("b", core)
    for k, out in ((a, xa), (b, xb), (2, x2)):
        out[0] = add(mine[NX + k], other[NX + k])
        out[1] = add(mine_2[k], other_2[k])
    pairs[0] = add(mine[NX], other[NX])
    pairs[1] = add(mine_2[0], other_2[0])
    for k, way in enumerate((a, b, 2, 0)):
        pairs[2 + k] = add(mine_0[way], other_0[way])


def sides_sum(*parts):
    return pl.pallas_call(
        sides_kernel,
        in_specs=[FULL] * 6,
        out_specs=[FULL] * 4,
        out_shape=[vmem(2, ROW, COLS)] * 3 + [vmem(6, ROW, COLS)],
        compiler_params=params(4),
        cost_estimate=TINY,
        name="sides_sum",
    )(*held(*parts))


def middle_kernel(pairs, xa, xb, x2, row, *outs):
    zb_out, z2_out, xa_out, xb_out, x2_out, own_out = outs
    _, _, core = place_of()
    for k, out in enumerate((zb_out, z2_out)):
        out[...] = add(pairs[k], xa[k], xb[k], x2[k])
    ways = (step("a", core), step("b", core), 2, 0)
    for k, out in enumerate((xa_out, xb_out, x2_out, own_out)):
        out[...] = add(pairs[2 + k], row[ways[k]])


def middle_sum(*parts):
    return pl.pallas_call(
        middle_kernel,
        in_specs=[FULL] * 5,
        out_specs=[FULL] * 6,
        out_shape=[vmem(ROW, COLS)] * 6,
        compiler_params=params(4),
        cost_estimate=TINY,
        name="middle_sum",
    )(*held(*parts))


def seen_kernel(*refs):
    refs[-1][...] = jnp.zeros_like(refs[-1])


def seen(*parts):
    return pl.pallas_call(
        seen_kernel,
        in_specs=[FULL] * len(parts),
        out_specs=FULL,
        out_shape=vmem(16, 128),
        compiler_params=params(1),
        cost_estimate=TINY,
        name="seen",
    )(*held(*parts))


def update_kernel(*refs):
    parts = refs[0:6]
    exps, signs, table, master, moment, second = refs[6:12]
    grad_out, moment_out, second_out, master_out, weights_out = refs[13:18]
    zh, x, core = place_of()
    lanes = pl.ds(pl.multiple_of((zh * NX + x) * GROUP, GROUP), GROUP)
    growth = jnp.exp2(exps[:, lanes].astype(F32)).T
    growth = jnp.where(core == 0, growth[:ROW], growth[ROW:])
    first_fix = 1.0 - beta_one**step_number
    second_fix = 1.0 - beta_two**step_number
    for tile in range(TILES):
        cut = slice(tile * TILE, (tile + 1) * TILE)
        total = parts[0][:, cut].astype(F32)
        for part in parts[1:]:
            total = total + part[:, cut].astype(F32)
        decoded = total * growth[:, tile : tile + 1]
        high = decoded.astype(BF)
        rest = decoded - high.astype(F32)
        middle = rest.astype(BF)
        low = (rest - middle.astype(F32)).astype(BF)
        restored = jnp.dot(high, table[...], preferred_element_type=F32) + (
            jnp.dot(middle, table[...], preferred_element_type=F32)
            + jnp.dot(low, table[...], preferred_element_type=F32)
        )
        grad = restored * (signs[:, cut].astype(F32) * (1.0 / REPLICAS))
        moment_new = beta_one * moment[:, cut] + (1.0 - beta_one) * grad
        second_new = beta_two * second[:, cut] + (1.0 - beta_two) * grad * grad
        update = (
            moment_new / first_fix / (jnp.sqrt(second_new / second_fix) + epsilon)
            + decay_rate * master[:, cut]
        )
        master_new = master[:, cut] - learn_rate * update
        weights_out[:, cut] = master_new.astype(BF)
        grad_out[:, cut] = grad
        moment_out[:, cut] = moment_new
        second_out[:, cut] = second_new
        master_out[:, cut] = master_new


def updated(parts, exps, signs, table, state, after):
    return pl.pallas_call(
        update_kernel,
        in_specs=[FULL] * 13,
        out_specs=[FULL] * 5,
        out_shape=[vmem(ROW, COLS, dtype=F32)] * 4 + [vmem(ROW, COLS)],
        compiler_params=params(4),
        cost_estimate=TINY,
        name="update",
    )(*held(*parts, exps, signs, table, *state, after))


def join_kernel(count, *refs):
    out = refs[-1]
    row = 0
    for part in refs[:count]:
        if len(part.shape) == 3:
            out[row : row + part.shape[0]] = part[...]
            row += part.shape[0]
        else:
            out[row] = part[...]
            row += 1


def joined(*parts, after=()):
    blocks = sum(part.shape[0] if part.ndim == 3 else 1 for part in parts)
    return pl.pallas_call(
        functools.partial(join_kernel, len(parts)),
        in_specs=[FULL] * (len(parts) + len(after)),
        out_specs=FULL,
        out_shape=vmem(blocks, ROW, COLS),
        compiler_params=params(2),
        cost_estimate=TINY,
        name="join",
    )(*held(*parts, *after))


def fan_kernel(w, xb, xa, x2, z2, za, _, column, row, first):
    for k, part in enumerate((za, z2)):
        column[k] = part[...]
    for k, part in enumerate((w, xa, xb, x2)):
        row[k] = part[...]
    for k, part in enumerate((w, za, z2, x2, xa, xb)):
        first[k] = part[...]


def fanned(*parts):
    return pl.pallas_call(
        fan_kernel,
        in_specs=[FULL] * 7,
        out_specs=[FULL] * 3,
        out_shape=[vmem(2, ROW, COLS), vmem(4, ROW, COLS), vmem(6, ROW, COLS)],
        compiler_params=params(2),
        cost_estimate=TINY,
        name="fan",
    )(*held(*parts))


def place_kernel(names, flips, count, chained, *refs):
    pieces = refs[: len(flips)]
    refs = refs[len(flips) :]
    state = refs[:count]
    out = refs[count + chained]
    state_out = refs[1 + count + chained : 1 + 2 * count + chained]
    token, sems = refs[-2:]
    token[...] = jnp.zeros_like(token)
    zh, x, core = place_of()
    copies = []
    for flip, piece in zip(flips, pieces):
        row_core = 1 - core if flip else core
        for k, (dx, dz) in enumerate(names):
            z_from = lax.rem(zh + NZ - step(dz, row_core), NZ)
            x_from = lax.rem(x + NX - step(dx, row_core), NX)
            row = pl.multiple_of(((z_from * NX + x_from) * NC + row_core) * ROW, ROW)
            copies.append(
                pltpu.make_async_copy(
                    piece.at[k], out.at[pl.ds(row, ROW), :], sems.at[len(copies)]
                )
            )
    for near, away in zip(state, state_out):
        copies.append(pltpu.make_async_copy(near, away, sems.at[len(copies)]))
    for copy in copies:
        copy.start()
    for copy in copies:
        copy.wait()


def placed(names, flips, pieces, state, previous):
    count = len(state)
    chained = previous is not None
    full = jax.ShapeDtypeStruct((ROW, COLS), F32)
    return pl.pallas_call(
        functools.partial(place_kernel, names, flips, count, chained),
        in_specs=[FULL] * (len(flips) + count) + [HBM] * chained,
        out_specs=[HBM] * (1 + count) + [FULL],
        out_shape=[jax.ShapeDtypeStruct((ROWS, COLS), BF)] + [full] * count + [vmem(16, 128)],
        input_output_aliases={len(flips) + count: 0} if chained else {},
        scratch_shapes=[pltpu.SemaphoreType.DMA((len(flips) * len(names) + count,))],
        compiler_params=params(2),
        cost_estimate=TINY,
        name="place",
    )(*held(*pieces, *state), *((previous,) if chained else ()))


def on_device(activations, out_grads, exponents, signs, master, moment, second_moment):
    table = jnp.asarray(hadamard_table(TILE), BF)
    mine, theirs, act, rotated, exps, sign_row, table = quantized_first(
        activations, out_grads, exponents.T, signs, table
    )
    other = send(theirs, dc=1)
    mine_2, theirs_2 = quantized_next(2, act, rotated, exps, theirs)
    other_2 = send(theirs_2, dc=1)
    mine_0, theirs_0 = quantized_next(0, act, rotated, exps, theirs_2)
    other_0 = send(theirs_0, dc=1)
    row = send(row_sum(mine, other, mine_0), dz="a")
    xa, xb, x2, pairs = sides_sum(mine, other, mine_2, other_2, mine_0, other_0)
    xa, xb, x2 = send(xa, dx="a"), send(xb, dx="b"), send(x2, dx=2)
    zb, z2, xa, xb, x2, own = middle_sum(pairs, xa, xb, x2, row)
    zb, z2 = send(zb, dz="b"), send(z2, dz=2)
    x2, xa, xb = send(x2, dx=2), send(xa, dx="a"), send(xb, dx="b")
    parts = [own, zb, z2, x2, xa, xb]
    token = seen(z2, zb)
    state = (master, moment, second_moment)
    *state_new, w = updated(parts, exps, sign_row, table, state, token)

    za, z2 = send(w, dz="a"), send(w, dz=2)
    x2, xa, xb = send(w, dx=2), send(w, dx="a"), send(w, dx="b")
    token = seen(z2, za)
    column, row, first = fanned(w, xb, xa, x2, z2, za, token)
    other_first = send(first, dc=1)
    zbr = send(row, dz="b")
    xac, xbc, x2c = send(column, dx="a"), send(column, dx="b"), send(column, dx=2)
    weights, *state_new, token = placed(
        FIRST_NAMES, (False, True), (first, other_first), state_new, None
    )
    last = joined(zbr, x2c, xbc, xac, after=(token,))
    other_last = send(last, dc=1)
    weights, _ = placed(LAST_NAMES, (False,), (last,), (), weights)
    weights, _ = placed(LAST_NAMES, (True,), (other_last,), (), weights)
    return (*state_new, weights)


def solution(mesh):
    in_specs = (
        P("replica", None),
        P("replica", "tensor"),
        P(None, "tensor"),
        P("tensor"),
        P("replica", "tensor"),
        P("replica", "tensor"),
        P("replica", "tensor"),
    )
    out_specs = (
        P("replica", "tensor"),
        P("replica", "tensor"),
        P("replica", "tensor"),
        P("replica", "tensor"),
        P(None, "tensor"),
    )
    return jax.shard_map(
        on_device, mesh=mesh, in_specs=in_specs, out_specs=out_specs, check_vma=False
    )
```

```python
import functools
import math

import jax
import jax.numpy as jnp
import numpy as np
from jax import lax
from jax.experimental import pallas as pl
from jax.experimental.pallas import tpu as pltpu
from jax.sharding import PartitionSpec as P

TILE = 256
NZ, NX, NC = 4, 4, 2
REPLICAS = NZ * NX * NC
ROW = 64
GROUP = NC * ROW
ROWS = NZ * NX * GROUP
COLS = 1280
TILES = COLS // TILE
TOK = 768

beta_one = 0.9
beta_two = 0.95
epsilon = 1e-08
decay_rate = 0.1
learn_rate = 0.001
step_number = 100.0

F32 = jnp.float32
BF = jnp.bfloat16
MIB = 1024 * 1024
HBM = pl.BlockSpec(memory_space=pltpu.HBM)
FULL = pl.BlockSpec(memory_space=pltpu.VMEM)

FIRST_NAMES = ((0, 0), (0, "a"), (0, 2), (2, 0), ("a", 0), ("b", 0))
LAST_NAMES = ((0, "b"), ("a", "b"), ("b", "b"), (2, "b"))
LAST_NAMES += ((2, "a"), (2, 2), ("b", "a"), ("b", 2), ("a", "a"), ("a", 2))


def hadamard_table(order):
    positions = np.arange(order)
    intersection = positions[:, None] & positions[None, :]
    parity = np.zeros((order, order))
    for level in range(order.bit_length()):
        parity = parity + intersection // 2**level % 2
    return np.where(parity % 2 == 0, 1.0, -1.0) / math.sqrt(order)


def step(way, core):
    if way == "a":
        return 1 + 2 * core
    if way == "b":
        return 3 - 2 * core
    return way


def replica_perm(dx, dz, dc):
    pairs = []
    for z in range(NZ):
        for x in range(NX):
            for c in range(NC):
                z_to, x_to = (z + step(dz, c)) % NZ, (x + step(dx, c)) % NX
                pairs.append(((z * NX + x) * NC + c, (z_to * NX + x_to) * NC + (c + dc) % NC))
    return pairs


def send(value, dx=0, dz=0, dc=0):
    return lax.ppermute(value, "replica", replica_perm(dx, dz, dc))


def place_of():
    replica = lax.axis_index("replica")
    return replica // (NX * NC), lax.rem(replica // NC, NX), lax.rem(replica, NC)


def vmem(*shape, dtype=BF):
    return pltpu.VMEM(shape, dtype)


def held(*arrays):
    return [pltpu.with_memory_space_constraint(a, pltpu.VMEM) for a in arrays]


def far(*arrays):
    return [pltpu.with_memory_space_constraint(a, pltpu.HBM) for a in arrays]


TINY = pl.CostEstimate(flops=1, bytes_accessed=1, transcendentals=0)


def params(mib):
    return pltpu.CompilerParams(vmem_limit_bytes=mib * MIB)


def quant_group(dx, dz, act, rotated, exps, mine, theirs):
    zh, x, core = place_of()
    group = lax.rem(zh + dz, NZ) * NX + lax.rem(x + dx, NX)
    lanes = pl.ds(pl.multiple_of(group * GROUP, GROUP), GROUP)
    total = lax.dot_general(
        act[:, lanes], rotated[...], (((0,), (0,)), ((), ())), preferred_element_type=F32
    )
    shrink = jnp.exp2(-exps[:, lanes].astype(F32)).T
    for tile in range(TILES):
        cut = slice(tile * TILE, (tile + 1) * TILE)
        part = jnp.clip(total[:, cut] * shrink[:, tile : tile + 1], -127.0, 127.0).astype(BF)
        top, bottom = part[:ROW], part[ROW:]
        mine[:, cut] = jnp.where(core == 0, top, bottom)
        theirs[:, cut] = jnp.where(core == 0, bottom, top)


def first_kernel(
    act_far, grads_far, exps_far, signs_far, table_far,
    mine, theirs, act, rotated, exps, signs, table,
    grads, line, sems,
):
    small = [
        pltpu.make_async_copy(signs_far, line, sems.at[0]),
        pltpu.make_async_copy(table_far, table, sems.at[1]),
        pltpu.make_async_copy(exps_far, exps, sems.at[2]),
    ]
    strips = []
    for far_ref, near, count in ((grads_far, grads, 3), (act_far, act, 4)):
        for k in range(count):
            rows = pl.ds(k * TOK // count, TOK // count)
            strips.append(
                pltpu.make_async_copy(far_ref.at[rows], near.at[rows], sems.at[3 + len(strips)])
            )
    for copy in small + strips:
        copy.start()
    for copy in small:
        copy.wait()
    signs[...] = line[...].reshape(1, COLS)
    for k in range(3):
        rows = slice(k * TOK // 3, (k + 1) * TOK // 3)
        strips[k].wait()
        for tile in range(TILES):
            cut = slice(tile * TILE, (tile + 1) * TILE)
            flipped = grads[rows, cut] * signs[:, cut].astype(BF)
            turned = jnp.dot(flipped, table[...], preferred_element_type=F32)
            rotated[rows, cut] = turned.astype(BF)
    for copy in strips[3:]:
        copy.wait()
    _, _, core = place_of()
    for dx in range(NX):
        here, there = mine.at[dx], theirs.at[NX + dx]
        quant_group(dx, step("a", core), act, rotated, exps, here, there)
        here, there = mine.at[NX + dx], theirs.at[dx]
        quant_group(dx, step("b", core), act, rotated, exps, here, there)


def quantized_first(act, grads, exps, signs, table):
    return pl.pallas_call(
        first_kernel,
        in_specs=[HBM] * 5,
        out_specs=[FULL] * 7,
        out_shape=[vmem(2 * NX, ROW, COLS)] * 2
        + [
            vmem(TOK, ROWS),
            vmem(TOK, COLS),
            vmem(TILES, ROWS, dtype=jnp.int32),
            vmem(1, COLS, dtype=jnp.int32),
            vmem(TILE, TILE),
        ],
        scratch_shapes=[
            pltpu.VMEM((TOK, COLS), BF),
            pltpu.VMEM((COLS,), jnp.int32),
            pltpu.SemaphoreType.DMA((10,)),
        ],
        compiler_params=params(12),
        cost_estimate=TINY,
        name="quantize_first",
    )(*far(act, grads, exps, signs, table))


def next_kernel(dz, act, rotated, exps, _, mine, theirs):
    for dx in range(NX):
        quant_group(dx, dz, act, rotated, exps, mine.at[dx], theirs.at[dx])


def quantized_next(dz, act, rotated, exps, after):
    return pl.pallas_call(
        functools.partial(next_kernel, dz),
        in_specs=[FULL] * 4,
        out_specs=[FULL] * 2,
        out_shape=[vmem(NX, ROW, COLS)] * 2,
        compiler_params=params(8),
        cost_estimate=TINY,
        name="quantize_next",
    )(*held(act, rotated, exps, after))


def add(*parts):
    total = parts[0].astype(F32)
    for part in parts[1:]:
        total = total + part.astype(F32)
    return total.astype(BF)


def row_kernel(mine, other, _, out):
    for k in range(NX):
        out[k] = add(mine[k], other[k])


def row_sum(mine, other, after):
    return pl.pallas_call(
        row_kernel,
        in_specs=[FULL] * 3,
        out_specs=FULL,
        out_shape=vmem(NX, ROW, COLS),
        compiler_params=params(2),
        cost_estimate=TINY,
        name="row_sum",
    )(*held(mine, other, after))


def sides_kernel(mine, other, mine_2, other_2, xa, xb, x2):
    _, _, core = place_of()
    a, b = step("a", core), step("b", core)
    for k, out in ((a, xa), (b, xb), (2, x2)):
        out[0] = add(mine[NX + k], other[NX + k])
        out[1] = add(mine_2[k], other_2[k])


def sides_sum(*parts):
    return pl.pallas_call(
        sides_kernel,
        in_specs=[FULL] * 4,
        out_specs=[FULL] * 3,
        out_shape=[vmem(2, ROW, COLS)] * 3,
        compiler_params=params(4),
        cost_estimate=TINY,
        name="sides_sum",
    )(*held(*parts))


def middle_kernel(mine, other, mine_2, other_2, mine_0, other_0, xa, xb, x2, row, *outs):
    zb_out, z2_out, xa_out, xb_out, x2_out, own_out = outs
    _, _, core = place_of()
    zb_out[...] = add(mine[NX], other[NX], xa[0], xb[0], x2[0])
    z2_out[...] = add(mine_2[0], other_2[0], xa[1], xb[1], x2[1])
    ways = (step("a", core), step("b", core), 2, 0)
    for way, out in zip(ways, (xa_out, xb_out, x2_out, own_out)):
        out[...] = add(mine_0[way], other_0[way], row[way])


def middle_sum(*parts):
    return pl.pallas_call(
        middle_kernel,
        in_specs=[FULL] * 10,
        out_specs=[FULL] * 6,
        out_shape=[vmem(ROW, COLS)] * 6,
        compiler_params=params(4),
        cost_estimate=TINY,
        name="middle_sum",
    )(*held(*parts))


def seen_kernel(*refs):
    refs[-1][...] = jnp.zeros_like(refs[-1])


def seen(*parts):
    return pl.pallas_call(
        seen_kernel,
        in_specs=[FULL] * len(parts),
        out_specs=FULL,
        out_shape=vmem(16, 128),
        compiler_params=params(1),
        cost_estimate=TINY,
        name="seen",
    )(*held(*parts))


def update_kernel(*refs):
    parts = refs[0:6]
    exps, signs, table, master, moment, second = refs[6:12]
    grad_out, moment_out, second_out, master_out, weights_out = refs[13:18]
    zh, x, core = place_of()
    lanes = pl.ds(pl.multiple_of((zh * NX + x) * GROUP, GROUP), GROUP)
    growth = jnp.exp2(exps[:, lanes].astype(F32)).T
    growth = jnp.where(core == 0, growth[:ROW], growth[ROW:])
    first_fix = 1.0 - beta_one**step_number
    second_fix = 1.0 - beta_two**step_number
    for tile in range(TILES):
        cut = slice(tile * TILE, (tile + 1) * TILE)
        total = parts[0][:, cut].astype(F32)
        for part in parts[1:]:
            total = total + part[:, cut].astype(F32)
        decoded = total * growth[:, tile : tile + 1]
        high = decoded.astype(BF)
        rest = decoded - high.astype(F32)
        middle = rest.astype(BF)
        low = (rest - middle.astype(F32)).astype(BF)
        restored = jnp.dot(high, table[...], preferred_element_type=F32) + (
            jnp.dot(middle, table[...], preferred_element_type=F32)
            + jnp.dot(low, table[...], preferred_element_type=F32)
        )
        grad = restored * (signs[:, cut].astype(F32) * (1.0 / REPLICAS))
        moment_new = beta_one * moment[:, cut] + (1.0 - beta_one) * grad
        second_new = beta_two * second[:, cut] + (1.0 - beta_two) * grad * grad
        update = (
            moment_new / first_fix / (jnp.sqrt(second_new / second_fix) + epsilon)
            + decay_rate * master[:, cut]
        )
        master_new = master[:, cut] - learn_rate * update
        weights_out[:, cut] = master_new.astype(BF)
        grad_out[:, cut] = grad
        moment_out[:, cut] = moment_new
        second_out[:, cut] = second_new
        master_out[:, cut] = master_new


def updated(parts, exps, signs, table, state, after):
    return pl.pallas_call(
        update_kernel,
        in_specs=[FULL] * 13,
        out_specs=[FULL] * 5,
        out_shape=[vmem(ROW, COLS, dtype=F32)] * 4 + [vmem(ROW, COLS)],
        compiler_params=params(4),
        cost_estimate=TINY,
        name="update",
    )(*held(*parts, exps, signs, table, *state, after))


def join_kernel(count, *refs):
    out = refs[-1]
    row = 0
    for part in refs[:count]:
        if len(part.shape) == 3:
            out[row : row + part.shape[0]] = part[...]
            row += part.shape[0]
        else:
            out[row] = part[...]
            row += 1


def joined(*parts, after=()):
    blocks = sum(part.shape[0] if part.ndim == 3 else 1 for part in parts)
    return pl.pallas_call(
        functools.partial(join_kernel, len(parts)),
        in_specs=[FULL] * (len(parts) + len(after)),
        out_specs=FULL,
        out_shape=vmem(blocks, ROW, COLS),
        compiler_params=params(2),
        cost_estimate=TINY,
        name="join",
    )(*held(*parts, *after))


def fan_kernel(w, xb, xa, x2, z2, za, _, column, row, first):
    for k, part in enumerate((za, z2)):
        column[k] = part[...]
    for k, part in enumerate((w, xa, xb, x2)):
        row[k] = part[...]
    for k, part in enumerate((w, za, z2, x2, xa, xb)):
        first[k] = part[...]


def fanned(*parts):
    return pl.pallas_call(
        fan_kernel,
        in_specs=[FULL] * 7,
        out_specs=[FULL] * 3,
        out_shape=[vmem(2, ROW, COLS), vmem(4, ROW, COLS), vmem(6, ROW, COLS)],
        compiler_params=params(2),
        cost_estimate=TINY,
        name="fan",
    )(*held(*parts))


def place_kernel(names, flips, count, chained, *refs):
    pieces = refs[: len(flips)]
    refs = refs[len(flips) :]
    state = refs[:count]
    out = refs[count + chained]
    state_out = refs[1 + count + chained : 1 + 2 * count + chained]
    token, sems = refs[-2:]
    token[...] = jnp.zeros_like(token)
    zh, x, core = place_of()
    copies = []
    for flip, piece in zip(flips, pieces):
        row_core = 1 - core if flip else core
        for k, (dx, dz) in enumerate(names):
            z_from = lax.rem(zh + NZ - step(dz, row_core), NZ)
            x_from = lax.rem(x + NX - step(dx, row_core), NX)
            row = pl.multiple_of(((z_from * NX + x_from) * NC + row_core) * ROW, ROW)
            copies.append(
                pltpu.make_async_copy(
                    piece.at[k], out.at[pl.ds(row, ROW), :], sems.at[len(copies)]
                )
            )
    for near, away in zip(state, state_out):
        copies.append(pltpu.make_async_copy(near, away, sems.at[len(copies)]))
    for copy in copies:
        copy.start()
    for copy in copies:
        copy.wait()


def placed(names, flips, pieces, state, previous):
    count = len(state)
    chained = previous is not None
    full = jax.ShapeDtypeStruct((ROW, COLS), F32)
    return pl.pallas_call(
        functools.partial(place_kernel, names, flips, count, chained),
        in_specs=[FULL] * (len(flips) + count) + [HBM] * chained,
        out_specs=[HBM] * (1 + count) + [FULL],
        out_shape=[jax.ShapeDtypeStruct((ROWS, COLS), BF)] + [full] * count + [vmem(16, 128)],
        input_output_aliases={len(flips) + count: 0} if chained else {},
        scratch_shapes=[pltpu.SemaphoreType.DMA((len(flips) * len(names) + count,))],
        compiler_params=params(2),
        cost_estimate=TINY,
        name="place",
    )(*held(*pieces, *state), *((previous,) if chained else ()))


def on_device(activations, out_grads, exponents, signs, master, moment, second_moment):
    table = jnp.asarray(hadamard_table(TILE), BF)
    mine, theirs, act, rotated, exps, sign_row, table = quantized_first(
        activations, out_grads, exponents.T, signs, table
    )
    other = send(theirs, dc=1)
    mine_2, theirs_2 = quantized_next(2, act, rotated, exps, theirs)
    other_2 = send(theirs_2, dc=1)
    mine_0, theirs_0 = quantized_next(0, act, rotated, exps, theirs_2)
    other_0 = send(theirs_0, dc=1)
    row = send(row_sum(mine, other, mine_0), dz="a")
    xa, xb, x2 = sides_sum(mine, other, mine_2, other_2)
    xa, xb, x2 = send(xa, dx="a"), send(xb, dx="b"), send(x2, dx=2)
    zb, z2, xa, xb, x2, own = middle_sum(
        mine, other, mine_2, other_2, mine_0, other_0, xa, xb, x2, row
    )
    zb, z2 = send(zb, dz="b"), send(z2, dz=2)
    x2, xa, xb = send(x2, dx=2), send(xa, dx="a"), send(xb, dx="b")
    parts = [own, zb, z2, x2, xa, xb]
    token = seen(z2, zb)
    state = (master, moment, second_moment)
    *state_new, w = updated(parts, exps, sign_row, table, state, token)

    za, z2 = send(w, dz="a"), send(w, dz=2)
    x2, xa, xb = send(w, dx=2), send(w, dx="a"), send(w, dx="b")
    token = seen(z2, za)
    column, row, first = fanned(w, xb, xa, x2, z2, za, token)
    other_first = send(first, dc=1)
    zbr = send(row, dz="b")
    xac, xbc, x2c = send(column, dx="a"), send(column, dx="b"), send(column, dx=2)
    weights, *state_new, token = placed(
        FIRST_NAMES, (False, True), (first, other_first), state_new, None
    )
    last = joined(zbr, x2c, xbc, xac, after=(token,))
    other_last = send(last, dc=1)
    weights, _ = placed(LAST_NAMES, (False,), (last,), (), weights)
    weights, _ = placed(LAST_NAMES, (True,), (other_last,), (), weights)
    return (*state_new, weights)


def solution(mesh):
    in_specs = (
        P("replica", None),
        P("replica", "tensor"),
        P(None, "tensor"),
        P("tensor"),
        P("replica", "tensor"),
        P("replica", "tensor"),
        P("replica", "tensor"),
    )
    out_specs = (
        P("replica", "tensor"),
        P("replica", "tensor"),
        P("replica", "tensor"),
        P("replica", "tensor"),
        P(None, "tensor"),
    )
    return jax.shard_map(
        on_device, mesh=mesh, in_specs=in_specs, out_specs=out_specs, check_vma=False
    )
```

```python
import functools
import math

import jax
import jax.numpy as jnp
import numpy as np
from jax import lax
from jax.experimental import pallas as pl
from jax.experimental.pallas import tpu as pltpu
from jax.sharding import PartitionSpec as P

TILE = 256
NZ, NX, NC = 4, 4, 2
REPLICAS = NZ * NX * NC
ROW = 64
GROUP = NC * ROW
ROWS = NZ * NX * GROUP
COLS = 1280
TILES = COLS // TILE
TOK = 768

beta_one = 0.9
beta_two = 0.95
epsilon = 1e-08
decay_rate = 0.1
learn_rate = 0.001
step_number = 100.0

F32 = jnp.float32
BF = jnp.bfloat16
MIB = 1024 * 1024
HBM = pl.BlockSpec(memory_space=pltpu.HBM)
FULL = pl.BlockSpec(memory_space=pltpu.VMEM)

FIRST_NAMES = ((0, 0), (0, "a"), (0, 2), (2, 0), ("a", 0), ("b", 0))
LAST_NAMES = ((0, "b"), ("a", "b"), ("b", "b"), (2, "b"))
LAST_NAMES += ((2, "a"), (2, 2), ("b", "a"), ("b", 2), ("a", "a"), ("a", 2))


def hadamard_table(order):
    positions = np.arange(order)
    intersection = positions[:, None] & positions[None, :]
    parity = np.zeros((order, order))
    for level in range(order.bit_length()):
        parity = parity + intersection // 2**level % 2
    return np.where(parity % 2 == 0, 1.0, -1.0) / math.sqrt(order)


def step(way, core):
    if way == "a":
        return 1 + 2 * core
    if way == "b":
        return 3 - 2 * core
    return way


def replica_perm(dx, dz, dc):
    pairs = []
    for z in range(NZ):
        for x in range(NX):
            for c in range(NC):
                z_to, x_to = (z + step(dz, c)) % NZ, (x + step(dx, c)) % NX
                pairs.append(((z * NX + x) * NC + c, (z_to * NX + x_to) * NC + (c + dc) % NC))
    return pairs


def send(value, dx=0, dz=0, dc=0):
    return lax.ppermute(value, "replica", replica_perm(dx, dz, dc))


def place_of():
    replica = lax.axis_index("replica")
    return replica // (NX * NC), lax.rem(replica // NC, NX), lax.rem(replica, NC)


def vmem(*shape, dtype=BF):
    return pltpu.VMEM(shape, dtype)


def held(*arrays):
    return [pltpu.with_memory_space_constraint(a, pltpu.VMEM) for a in arrays]


def far(*arrays):
    return [pltpu.with_memory_space_constraint(a, pltpu.HBM) for a in arrays]


TINY = pl.CostEstimate(flops=1, bytes_accessed=1, transcendentals=0)


def params(mib):
    return pltpu.CompilerParams(vmem_limit_bytes=mib * MIB)


def quant_group(dx, dz, act, rotated, exps, mine, theirs):
    zh, x, core = place_of()
    group = lax.rem(zh + dz, NZ) * NX + lax.rem(x + dx, NX)
    lanes = pl.ds(pl.multiple_of(group * GROUP, GROUP), GROUP)
    total = lax.dot_general(
        act[:, lanes], rotated[...], (((0,), (0,)), ((), ())), preferred_element_type=F32
    )
    shrink = jnp.exp2(-exps[:, lanes].astype(F32)).T
    for tile in range(TILES):
        cut = slice(tile * TILE, (tile + 1) * TILE)
        part = jnp.clip(total[:, cut] * shrink[:, tile : tile + 1], -127.0, 127.0).astype(BF)
        top, bottom = part[:ROW], part[ROW:]
        mine[:, cut] = jnp.where(core == 0, top, bottom)
        theirs[:, cut] = jnp.where(core == 0, bottom, top)


def first_kernel(
    act_far, grads_far, exps_far, signs_far, table_far,
    mine, theirs, act, rotated, exps, signs, table,
    grads, line, sems,
):
    small = [
        pltpu.make_async_copy(signs_far, line, sems.at[0]),
        pltpu.make_async_copy(table_far, table, sems.at[1]),
        pltpu.make_async_copy(exps_far, exps, sems.at[2]),
    ]
    strips = []
    for far_ref, near, count in ((grads_far, grads, 3), (act_far, act, 4)):
        for k in range(count):
            rows = pl.ds(k * TOK // count, TOK // count)
            strips.append(
                pltpu.make_async_copy(far_ref.at[rows], near.at[rows], sems.at[3 + len(strips)])
            )
    for copy in small + strips:
        copy.start()
    for copy in small:
        copy.wait()
    signs[...] = line[...].reshape(1, COLS)
    for k in range(3):
        rows = slice(k * TOK // 3, (k + 1) * TOK // 3)
        strips[k].wait()
        for tile in range(TILES):
            cut = slice(tile * TILE, (tile + 1) * TILE)
            flipped = grads[rows, cut] * signs[:, cut].astype(BF)
            turned = jnp.dot(flipped, table[...], preferred_element_type=F32)
            rotated[rows, cut] = turned.astype(BF)
    for copy in strips[3:]:
        copy.wait()
    _, _, core = place_of()
    for dx in range(NX):
        here, there = mine.at[dx], theirs.at[NX + dx]
        quant_group(dx, step("a", core), act, rotated, exps, here, there)
        here, there = mine.at[NX + dx], theirs.at[dx]
        quant_group(dx, step("b", core), act, rotated, exps, here, there)


def quantized_first(act, grads, exps, signs, table):
    return pl.pallas_call(
        first_kernel,
        in_specs=[HBM] * 5,
        out_specs=[FULL] * 7,
        out_shape=[vmem(2 * NX, ROW, COLS)] * 2
        + [
            vmem(TOK, ROWS),
            vmem(TOK, COLS),
            vmem(TILES, ROWS, dtype=jnp.int32),
            vmem(1, COLS, dtype=jnp.int32),
            vmem(TILE, TILE),
        ],
        scratch_shapes=[
            pltpu.VMEM((TOK, COLS), BF),
            pltpu.VMEM((COLS,), jnp.int32),
            pltpu.SemaphoreType.DMA((10,)),
        ],
        compiler_params=params(12),
        cost_estimate=TINY,
        name="quantize_first",
    )(*far(act, grads, exps, signs, table))


def next_kernel(dz, act, rotated, exps, _, mine, theirs):
    for dx in range(NX):
        quant_group(dx, dz, act, rotated, exps, mine.at[dx], theirs.at[dx])


def quantized_next(dz, act, rotated, exps, after):
    return pl.pallas_call(
        functools.partial(next_kernel, dz),
        in_specs=[FULL] * 4,
        out_specs=[FULL] * 2,
        out_shape=[vmem(NX, ROW, COLS)] * 2,
        compiler_params=params(8),
        cost_estimate=TINY,
        name="quantize_next",
    )(*held(act, rotated, exps, after))


def add(*parts):
    total = parts[0].astype(F32)
    for part in parts[1:]:
        total = total + part.astype(F32)
    return total.astype(BF)


def row_kernel(mine, other, _, out):
    for k in range(NX):
        out[k] = add(mine[k], other[k])


def row_sum(mine, other, after):
    return pl.pallas_call(
        row_kernel,
        in_specs=[FULL] * 3,
        out_specs=FULL,
        out_shape=vmem(NX, ROW, COLS),
        compiler_params=params(2),
        cost_estimate=TINY,
        name="row_sum",
    )(*held(mine, other, after))


def sides_kernel(mine, other, mine_2, other_2, xa, xb, x2):
    _, _, core = place_of()
    a, b = step("a", core), step("b", core)
    for k, out in ((a, xa), (b, xb), (2, x2)):
        out[0] = add(mine[NX + k], other[NX + k])
        out[1] = add(mine_2[k], other_2[k])


def sides_sum(*parts):
    return pl.pallas_call(
        sides_kernel,
        in_specs=[FULL] * 4,
        out_specs=[FULL] * 3,
        out_shape=[vmem(2, ROW, COLS)] * 3,
        compiler_params=params(4),
        cost_estimate=TINY,
        name="sides_sum",
    )(*held(*parts))


def middle_kernel(mine, other, mine_2, other_2, mine_0, other_0, x2, xa, xb, row, *outs):
    zb_out, z2_out, xa_out, xb_out, x2_out, own_out = outs
    _, _, core = place_of()
    zb_out[...] = add(mine[NX], other[NX], xa[0], xb[0], x2[0])
    z2_out[...] = add(mine_2[0], other_2[0], xa[1], xb[1], x2[1])
    ways = (step("a", core), step("b", core), 2, 0)
    for way, out in zip(ways, (xa_out, xb_out, x2_out, own_out)):
        out[...] = add(mine_0[way], other_0[way], row[way])


def middle_sum(*parts):
    return pl.pallas_call(
        middle_kernel,
        in_specs=[FULL] * 10,
        out_specs=[FULL] * 6,
        out_shape=[vmem(ROW, COLS)] * 6,
        compiler_params=params(4),
        cost_estimate=TINY,
        name="middle_sum",
    )(*held(*parts))


def seen_kernel(*refs):
    refs[-1][...] = jnp.zeros_like(refs[-1])


def seen(*parts):
    return pl.pallas_call(
        seen_kernel,
        in_specs=[FULL] * len(parts),
        out_specs=FULL,
        out_shape=vmem(16, 128),
        compiler_params=params(1),
        cost_estimate=TINY,
        name="seen",
    )(*held(*parts))


def update_kernel(*refs):
    parts = refs[0:6]
    exps, signs, table, master, moment, second = refs[6:12]
    grad_out, moment_out, second_out, master_out, weights_out = refs[13:18]
    zh, x, core = place_of()
    lanes = pl.ds(pl.multiple_of((zh * NX + x) * GROUP, GROUP), GROUP)
    growth = jnp.exp2(exps[:, lanes].astype(F32)).T
    growth = jnp.where(core == 0, growth[:ROW], growth[ROW:])
    first_fix = 1.0 - beta_one**step_number
    second_fix = 1.0 - beta_two**step_number
    for tile in range(TILES):
        cut = slice(tile * TILE, (tile + 1) * TILE)
        total = parts[0][:, cut].astype(F32)
        for part in parts[1:]:
            total = total + part[:, cut].astype(F32)
        decoded = total * growth[:, tile : tile + 1]
        high = decoded.astype(BF)
        rest = decoded - high.astype(F32)
        middle = rest.astype(BF)
        low = (rest - middle.astype(F32)).astype(BF)
        restored = jnp.dot(high, table[...], preferred_element_type=F32) + (
            jnp.dot(middle, table[...], preferred_element_type=F32)
            + jnp.dot(low, table[...], preferred_element_type=F32)
        )
        grad = restored * (signs[:, cut].astype(F32) * (1.0 / REPLICAS))
        moment_new = beta_one * moment[:, cut] + (1.0 - beta_one) * grad
        second_new = beta_two * second[:, cut] + (1.0 - beta_two) * grad * grad
        update = (
            moment_new / first_fix / (jnp.sqrt(second_new / second_fix) + epsilon)
            + decay_rate * master[:, cut]
        )
        master_new = master[:, cut] - learn_rate * update
        weights_out[:, cut] = master_new.astype(BF)
        grad_out[:, cut] = grad
        moment_out[:, cut] = moment_new
        second_out[:, cut] = second_new
        master_out[:, cut] = master_new


def updated(parts, exps, signs, table, state, after):
    return pl.pallas_call(
        update_kernel,
        in_specs=[FULL] * 13,
        out_specs=[FULL] * 5,
        out_shape=[vmem(ROW, COLS, dtype=F32)] * 4 + [vmem(ROW, COLS)],
        compiler_params=params(4),
        cost_estimate=TINY,
        name="update",
    )(*held(*parts, exps, signs, table, *state, after))


def join_kernel(count, *refs):
    out = refs[-1]
    row = 0
    for part in refs[:count]:
        if len(part.shape) == 3:
            out[row : row + part.shape[0]] = part[...]
            row += part.shape[0]
        else:
            out[row] = part[...]
            row += 1


def joined(*parts, after=()):
    blocks = sum(part.shape[0] if part.ndim == 3 else 1 for part in parts)
    return pl.pallas_call(
        functools.partial(join_kernel, len(parts)),
        in_specs=[FULL] * (len(parts) + len(after)),
        out_specs=FULL,
        out_shape=vmem(blocks, ROW, COLS),
        compiler_params=params(2),
        cost_estimate=TINY,
        name="join",
    )(*held(*parts, *after))


def fan_kernel(w, xb, xa, x2, z2, za, _, column, row, first):
    for k, part in enumerate((za, z2)):
        column[k] = part[...]
    for k, part in enumerate((w, xa, xb, x2)):
        row[k] = part[...]
    for k, part in enumerate((w, za, z2, x2, xa, xb)):
        first[k] = part[...]


def fanned(*parts):
    return pl.pallas_call(
        fan_kernel,
        in_specs=[FULL] * 7,
        out_specs=[FULL] * 3,
        out_shape=[vmem(2, ROW, COLS), vmem(4, ROW, COLS), vmem(6, ROW, COLS)],
        compiler_params=params(2),
        cost_estimate=TINY,
        name="fan",
    )(*held(*parts))


def place_kernel(names, flips, count, chained, *refs):
    pieces = refs[: len(flips)]
    refs = refs[len(flips) :]
    state = refs[:count]
    out = refs[count + chained]
    state_out = refs[1 + count + chained : 1 + 2 * count + chained]
    token, sems = refs[-2:]
    token[...] = jnp.zeros_like(token)
    zh, x, core = place_of()
    copies = []
    for flip, piece in zip(flips, pieces):
        row_core = 1 - core if flip else core
        for k, (dx, dz) in enumerate(names):
            z_from = lax.rem(zh + NZ - step(dz, row_core), NZ)
            x_from = lax.rem(x + NX - step(dx, row_core), NX)
            row = pl.multiple_of(((z_from * NX + x_from) * NC + row_core) * ROW, ROW)
            copies.append(
                pltpu.make_async_copy(
                    piece.at[k], out.at[pl.ds(row, ROW), :], sems.at[len(copies)]
                )
            )
    for near, away in zip(state, state_out):
        copies.append(pltpu.make_async_copy(near, away, sems.at[len(copies)]))
    for copy in copies:
        copy.start()
    for copy in copies:
        copy.wait()


def placed(names, flips, pieces, state, previous):
    count = len(state)
    chained = previous is not None
    full = jax.ShapeDtypeStruct((ROW, COLS), F32)
    return pl.pallas_call(
        functools.partial(place_kernel, names, flips, count, chained),
        in_specs=[FULL] * (len(flips) + count) + [HBM] * chained,
        out_specs=[HBM] * (1 + count) + [FULL],
        out_shape=[jax.ShapeDtypeStruct((ROWS, COLS), BF)] + [full] * count + [vmem(16, 128)],
        input_output_aliases={len(flips) + count: 0} if chained else {},
        scratch_shapes=[pltpu.SemaphoreType.DMA((len(flips) * len(names) + count,))],
        compiler_params=params(2),
        cost_estimate=TINY,
        name="place",
    )(*held(*pieces, *state), *((previous,) if chained else ()))


def on_device(activations, out_grads, exponents, signs, master, moment, second_moment):
    table = jnp.asarray(hadamard_table(TILE), BF)
    mine, theirs, act, rotated, exps, sign_row, table = quantized_first(
        activations, out_grads, exponents.T, signs, table
    )
    other = send(theirs, dc=1)
    mine_2, theirs_2 = quantized_next(2, act, rotated, exps, theirs)
    other_2 = send(theirs_2, dc=1)
    mine_0, theirs_0 = quantized_next(0, act, rotated, exps, theirs_2)
    other_0 = send(theirs_0, dc=1)
    row = send(row_sum(mine, other, mine_0), dz="a")
    xa, xb, x2 = sides_sum(mine, other, mine_2, other_2)
    xa, xb, x2 = send(xa, dx="a"), send(xb, dx="b"), send(x2, dx=2)
    zb, z2, xa, xb, x2, own = middle_sum(
        mine, other, mine_2, other_2, mine_0, other_0, x2, xa, xb, row
    )
    zb, z2 = send(zb, dz="b"), send(z2, dz=2)
    x2, xa, xb = send(x2, dx=2), send(xa, dx="a"), send(xb, dx="b")
    parts = [own, zb, z2, x2, xa, xb]
    token = seen(z2, zb)
    state = (master, moment, second_moment)
    *state_new, w = updated(parts, exps, sign_row, table, state, token)

    za, z2 = send(w, dz="a"), send(w, dz=2)
    x2, xa, xb = send(w, dx=2), send(w, dx="a"), send(w, dx="b")
    token = seen(z2, za)
    column, row, first = fanned(w, xb, xa, x2, z2, za, token)
    other_first = send(first, dc=1)
    zbr = send(row, dz="b")
    xac, xbc, x2c = send(column, dx="a"), send(column, dx="b"), send(column, dx=2)
    weights, *state_new, token = placed(
        FIRST_NAMES, (False, True), (first, other_first), state_new, None
    )
    last = joined(zbr, x2c, xbc, xac, after=(token,))
    other_last = send(last, dc=1)
    weights, _ = placed(LAST_NAMES, (False,), (last,), (), weights)
    weights, _ = placed(LAST_NAMES, (True,), (other_last,), (), weights)
    return (*state_new, weights)


def solution(mesh):
    in_specs = (
        P("replica", None),
        P("replica", "tensor"),
        P(None, "tensor"),
        P("tensor"),
        P("replica", "tensor"),
        P("replica", "tensor"),
        P("replica", "tensor"),
    )
    out_specs = (
        P("replica", "tensor"),
        P("replica", "tensor"),
        P("replica", "tensor"),
        P("replica", "tensor"),
        P(None, "tensor"),
    )
    return jax.shard_map(
        on_device, mesh=mesh, in_specs=in_specs, out_specs=out_specs, check_vma=False
    )
```
